32 devices in a mesh: ctx: 4 (over z), fsdp: 4 (over y, x), replica: 2 (over core).
Axes of the slice: x: 2, y: 2, z: 4, core: 2. Of those that a mesh axis runs over, the one named last changes fastest.
Arguments:
- tokens: bfloat16 [8, 512, 1024], P(('fsdp', 'replica'), 'ctx'), may hold values from -6 to 6
- output_gradient: bfloat16 [8, 512, 1024], P(('fsdp', 'replica'), 'ctx'), may hold values from -6 to 6
- segment_ids: int32 [8, 512], P(('fsdp', 'replica')), may hold values from 0 to 2, as said below
- row_fill: int32 [8], P(('fsdp', 'replica')), may hold values from 256 to 512, as said below
- w_qkv: float32 [1024, 3072], P(('ctx', 'fsdp')), may hold values from -0.1875 to 0.1875
- w_attn_out: float32 [1024, 1024], P(('ctx', 'fsdp')), may hold values from -0.5 to 0.5
- w_up: float32 [1024, 4096], P(('ctx', 'fsdp')), may hold values from -0.1875 to 0.1875
- w_down: float32 [4096, 1024], P(('ctx', 'fsdp')), may hold values from -0.09375 to 0.09375
- vectors: float32 [13312], P(('ctx', 'fsdp')), may hold values from -0.5 to 1.4, as said below
- momentum_qkv_weight: float32 [1024, 3072], P(('ctx', 'fsdp')), may hold values from -80 to 80
- momentum_attn_output: float32 [1024, 1024], P(('ctx', 'fsdp')), may hold values from -16 to 16
- momentum_up_weight: float32 [1024, 4096], P(('ctx', 'fsdp')), may hold values from -10 to 10
- momentum_down_weight: float32 [4096, 1024], P(('ctx', 'fsdp')), may hold values from -24 to 24
- momentum_vector_rows: float32 [13312], P(('ctx', 'fsdp')), may hold values from -40 to 40
- second_qkv: float32 [1024, 3072], P(('ctx', 'fsdp')), may hold values from 860.16 to 3440.64
- second_attn_out: float32 [1024, 1024], P(('ctx', 'fsdp')), may hold values from 34.4064 to 139.264
- second_up: float32 [1024, 4096], P(('ctx', 'fsdp')), may hold values from 12.94336 to 51.6096
- second_down: float32 [4096, 1024], P(('ctx', 'fsdp')), may hold values from 64.7168 to 258.048
- second_vectors: float32 [13312], P(('ctx', 'fsdp')), may hold values from 215.4496 to 860.16
Outputs:
- block_out: bfloat16 [8, 512, 1024], P(('fsdp', 'replica'), 'ctx')
- tokens_grad: float32 [8, 512, 1024], P(('fsdp', 'replica'), 'ctx')
- next_qkv: float32 [1024, 3072], P(('ctx', 'fsdp'))
- next_attn_out: float32 [1024, 1024], P(('ctx', 'fsdp'))
- next_up: float32 [1024, 4096], P(('ctx', 'fsdp'))
- next_down: float32 [4096, 1024], P(('ctx', 'fsdp'))
- next_vectors: float32 [13312], P(('ctx', 'fsdp'))
- next_first_qkv: float32 [1024, 3072], P(('ctx', 'fsdp'))
- next_first_attn_out: float32 [1024, 1024], P(('ctx', 'fsdp'))
- next_first_up: float32 [1024, 4096], P(('ctx', 'fsdp'))
- next_first_down: float32 [4096, 1024], P(('ctx', 'fsdp'))
- next_first_vectors: float32 [13312], P(('ctx', 'fsdp'))
- next_second_qkv: float32 [1024, 3072], P(('ctx', 'fsdp'))
- next_second_attn_out: float32 [1024, 1024], P(('ctx', 'fsdp'))
- next_second_up: float32 [1024, 4096], P(('ctx', 'fsdp'))
- next_second_down: float32 [4096, 1024], P(('ctx', 'fsdp'))
- next_second_vectors: float32 [13312], P(('ctx', 'fsdp'))
The draws below stay inside these ranges and needn't reach their ends.
Inputs may be any that keep to these rules, and one draw needn't show every extreme that they name: `segment_ids`: each row holds three documents numbered 0, 1, 2 in order of position; document 0 ends within the first eighth of the row and document 2 begins within the last eighth. `row_fill`: some row is full and some row is live on exactly half of its positions. `vectors`: entries of g1 and g2 lie in 0.6 to 1.4; the other entries lie in -0.5 to 0.5.
All inputs are finite; a program needn't handle non-finite values.
Results may differ from the reference program's by a relative error of at most 0.012.
Values may be sent and summed in bfloat16 or wider, within the bound.
A program may use at most 256 MiB of HBM per device.

```python
import math
import jax
import jax.numpy as jnp
from jax import lax

MODEL_WIDTH = 1024
HEADS = 16
HEAD_DIM = 64
HIDDEN_UNITS = 4096
PACKED_LENGTH = 512
STEP = 10
PACKED_ROWS = 8
VECTOR_COUNT = 13312


def draw_segment_ids(key, part):
    key = jax.random.fold_in(key, 3)
    leading_seed, trailing_seed = jax.random.split(key)
    initial_stop = jax.random.randint(leading_seed, (PACKED_ROWS, 1), 1, PACKED_LENGTH // 8 + 1)
    final_opening = jax.random.randint(trailing_seed, (PACKED_ROWS, 1), PACKED_LENGTH - PACKED_LENGTH // 8, PACKED_LENGTH)
    slot_numbers = jnp.arange(PACKED_LENGTH, dtype=jnp.int32)[None, :]
    return (slot_numbers >= initial_stop).astype(jnp.int32) + (slot_numbers >= final_opening).astype(jnp.int32)


def draw_row_fill(key, part):
    key = jax.random.fold_in(key, 5)
    filler_seed, full_key, half_key = jax.random.split(key, 3)
    filler_values = jax.random.randint(filler_seed, (PACKED_ROWS,), PACKED_LENGTH // 2, PACKED_LENGTH + 1)
    picked_entries = jax.random.randint(full_key, (), 0, PACKED_ROWS)
    remaining_part = (picked_entries + 1 + jax.random.randint(half_key, (), 0, PACKED_ROWS - 1)) % PACKED_ROWS
    packed_row_index = jnp.arange(PACKED_ROWS, dtype=jnp.int32)
    filler_values = jnp.where(packed_row_index == picked_entries, PACKED_LENGTH, filler_values)
    filler_values = jnp.where(packed_row_index == remaining_part, PACKED_LENGTH // 2, filler_values)
    return filler_values.astype(jnp.int32)


def draw_vectors(key, part):
    key = jax.random.fold_in(key, 7)
    gain_key, shift_key = jax.random.split(key)
    total_len = 9 * MODEL_WIDTH + HIDDEN_UNITS
    slot_numbers = jnp.arange(total_len, dtype=jnp.int32)
    is_gain = (slot_numbers < MODEL_WIDTH) | (slot_numbers >= 6 * MODEL_WIDTH) & (slot_numbers < 7 * MODEL_WIDTH)
    gain_vals = jax.random.uniform(gain_key, (total_len,), jnp.float32, 0.6, 1.4)
    shifts = 0.1 * jax.random.truncated_normal(shift_key, -5.0, 5.0, (total_len,), jnp.float32)
    return jnp.where(is_gain, gain_vals, shifts).astype(jnp.float32)


def level_of(own_key, dims, shards, least, top_value):
    def one(axis_at, parts):
        steps = jax.random.uniform(jax.random.fold_in(jax.random.fold_in(own_key, 6), axis_at), (parts,), jnp.float32, least / len(shards), top_value / len(shards))
        return jnp.repeat(jnp.exp(steps), dims[axis_at] // parts).reshape((-1,) + (1,) * (len(dims) - axis_at - 1))

    level = one(*shards[0])
    for cut in shards[1:]:
        level = level * one(*cut)
    return level


def scatter_about(key, extent, width, most, cuts=(), kind=jnp.bfloat16):
    values = jax.random.normal(key, extent, jnp.float32) * width
    if len(cuts) > 0:
        values = level_of(key, extent, cuts, -0.22, 0.18) * values
    return jnp.clip(values, min=-most, max=most).astype(kind)


def setup_inputs(seed: int = 0) -> dict:
    seeds = jax.random.split(jax.random.key(seed), 20)
    return {
        "tokens": scatter_about(seeds[0], (PACKED_ROWS, PACKED_LENGTH, MODEL_WIDTH), 1.0, 6.0, ((0, 8), (1, 4))),
        "output_gradient": scatter_about(seeds[1], (PACKED_ROWS, PACKED_LENGTH, MODEL_WIDTH), 1.0, 6.0, ((0, 8), (1, 4))),
        "segment_ids": draw_segment_ids(jax.random.fold_in(seeds[19], 71), 0),
        "row_fill": draw_row_fill(jax.random.fold_in(seeds[19], 71), 0),
        "w_qkv": scatter_about(seeds[4], (MODEL_WIDTH, 3 * MODEL_WIDTH), MODEL_WIDTH ** -0.5, 0.1875, ((0, 16),), jnp.float32),
        "w_attn_out": scatter_about(seeds[5], (MODEL_WIDTH, MODEL_WIDTH), (MODEL_WIDTH // 8) ** -0.5, 0.5, ((0, 16),), jnp.float32),
        "w_up": scatter_about(seeds[6], (MODEL_WIDTH, HIDDEN_UNITS), MODEL_WIDTH ** -0.5, 0.1875, ((0, 16),), jnp.float32),
        "w_down": scatter_about(seeds[7], (HIDDEN_UNITS, MODEL_WIDTH), HIDDEN_UNITS ** -0.5, 0.09375, ((0, 16),), jnp.float32),
        "vectors": draw_vectors(jax.random.fold_in(seeds[19], 71), 0),
        "momentum_qkv_weight": scatter_about(seeds[9], (MODEL_WIDTH, 3 * MODEL_WIDTH), (0.222 * (PACKED_ROWS * PACKED_LENGTH) ** 0.5), 80.0, ((0, 16),), jnp.float32),
        "momentum_attn_output": scatter_about(seeds[10], (MODEL_WIDTH, MODEL_WIDTH), (0.0444 * (PACKED_ROWS * PACKED_LENGTH) ** 0.5), 16.0, ((0, 16),), jnp.float32),
        "momentum_up_weight": scatter_about(seeds[11], (MODEL_WIDTH, HIDDEN_UNITS), (0.0272 * (PACKED_ROWS * PACKED_LENGTH) ** 0.5), 10.0, ((0, 16),), jnp.float32),
        "momentum_down_weight": scatter_about(seeds[12], (HIDDEN_UNITS, MODEL_WIDTH), (0.0608 * (PACKED_ROWS * PACKED_LENGTH) ** 0.5), 24.0, ((0, 16),), jnp.float32),
        "momentum_vector_rows": scatter_about(seeds[13], (VECTOR_COUNT,), (0.111 * (PACKED_ROWS * PACKED_LENGTH) ** 0.5), 40.0, ((0, 16),), jnp.float32),
        "second_qkv": jnp.clip(jnp.exp(math.log(3440.64) - 1.3862944 * jax.random.uniform(seeds[14], (MODEL_WIDTH, 3 * MODEL_WIDTH), jnp.float32) ** level_of(seeds[14], (MODEL_WIDTH, 3 * MODEL_WIDTH), ((0, 16),), -0.2, 0.2)), 860.16, 3440.64),
        "second_attn_out": jnp.clip(jnp.exp(math.log(139.264) - 1.3981289 * jax.random.uniform(seeds[15], (MODEL_WIDTH, MODEL_WIDTH), jnp.float32) ** level_of(seeds[15], (MODEL_WIDTH, MODEL_WIDTH), ((0, 16),), -0.2, 0.2)), 34.4064, 139.264),
        "second_up": jnp.clip(jnp.exp(math.log(51.6096) - 1.38312476 * jax.random.uniform(seeds[16], (MODEL_WIDTH, HIDDEN_UNITS), jnp.float32) ** level_of(seeds[16], (MODEL_WIDTH, HIDDEN_UNITS), ((0, 16),), -0.2, 0.2)), 12.94336, 51.6096),
        "second_down": jnp.clip(jnp.exp(math.log(258.048) - 1.38312485 * jax.random.uniform(seeds[17], (HIDDEN_UNITS, MODEL_WIDTH), jnp.float32) ** level_of(seeds[17], (HIDDEN_UNITS, MODEL_WIDTH), ((0, 16),), -0.2, 0.2)), 64.7168, 258.048),
        "second_vectors": jnp.clip(jnp.exp(math.log(860.16) - 1.3843914 * jax.random.uniform(seeds[18], (VECTOR_COUNT,), jnp.float32) ** level_of(seeds[18], (VECTOR_COUNT,), ((0, 16),), -0.2, 0.2)), 215.4496, 860.16),
    }


@jax.custom_vjp
def low(v):
    return lax.optimization_barrier(v.astype(jnp.bfloat16)).astype(jnp.float32)

@jax.custom_vjp
def low_back(v):
    return v

def low_keep(v):
    return (low(v), None)

def low_pass(kept, grad):
    return (grad,)

def back_keep(v):
    return (v, None)

def back_low(kept, grad):
    return (low(grad),)
low.defvjp(low_keep, low_pass)
low_back.defvjp(back_keep, back_low)
highest = lax.Precision.HIGHEST
norm_eps = 1e-05
score_scale = 0.125
masked_score = -1e+30
gelu_coef = 0.7978845608028654
beta_one = 0.9
beta_two = 0.95
adam_eps = 1e-08

def layer_norm(inputs, scale_vec, shift_vec):
    centre = inputs - lax.optimization_barrier(jnp.mean(inputs, axis=-1, keepdims=True))
    spread = lax.optimization_barrier(jnp.mean(centre * centre, axis=-1, keepdims=True))
    return centre * lax.rsqrt(spread + norm_eps) * scale_vec + shift_vec

def gelu_tanh(points):
    return 0.5 * points * (1.0 + jnp.tanh(gelu_coef * (points + 0.044715 * points * points * points)))

def alibi_slopes(count_heads):
    return jnp.power(2.0, -8.0 * (jnp.arange(count_heads, dtype=jnp.float32) + 1.0) / count_heads)

def split_small(vector_all):
    bounds = [0, MODEL_WIDTH, 2 * MODEL_WIDTH, 5 * MODEL_WIDTH, 6 * MODEL_WIDTH, 7 * MODEL_WIDTH, 8 * MODEL_WIDTH, 8 * MODEL_WIDTH + HIDDEN_UNITS, 9 * MODEL_WIDTH + HIDDEN_UNITS]
    return tuple((vector_all[low_end:high_end] for low_end, high_end in zip(bounds[:-1], bounds[1:])))

def attention_rows(queries, keys_all, values_all, seg_rows):
    row_len = queries.shape[1]
    slot_numbers = jnp.arange(row_len, dtype=jnp.int32)
    distance = (slot_numbers[:, None] - slot_numbers[None, :]).astype(jnp.float32)
    alibi_bias = -alibi_slopes(HEADS)[:, None, None] * distance[None, :, :]
    causal = slot_numbers[None, :] <= slot_numbers[:, None]
    same_doc = seg_rows[:, :, None] == seg_rows[:, None, :]
    allowed = (causal[None, :, :] & same_doc)[:, None, :, :]
    scores = jnp.einsum('rqhd,rkhd->rhqk', queries, keys_all, precision=highest) * score_scale + alibi_bias[None]
    scores = jnp.where(allowed, low_back(scores), masked_score)
    row_max = lax.optimization_barrier(jnp.max(scores, axis=-1, keepdims=True))
    exp_scores = jnp.exp(scores - row_max)
    prob_vals = low(exp_scores / lax.optimization_barrier(jnp.sum(exp_scores, axis=-1, keepdims=True)))
    return jnp.einsum('rhqk,rkhd->rqhd', prob_vals, values_all, precision=highest)

def block_rows(weights, row_vals, seg_rows):
    mat_qkv, mat_out, mat_up, mat_down, gain_one, shift_one, bias_qkv, bias_out, gain_two, shift_two, bias_up, bias_down = weights
    row_count, row_len = (row_vals.shape[0], row_vals.shape[1])
    hidden_one = low(layer_norm(row_vals, gain_one, shift_one))
    qkv_vals = jnp.einsum('rld,de->rle', hidden_one, mat_qkv, precision=highest) + bias_qkv
    qkv_vals = low(low_back(qkv_vals))
    head_shape = (row_count, row_len, HEADS, HEAD_DIM)
    queries = qkv_vals[:, :, :MODEL_WIDTH].reshape(head_shape)
    keys_all = qkv_vals[:, :, MODEL_WIDTH:2 * MODEL_WIDTH].reshape(head_shape)
    values_all = qkv_vals[:, :, 2 * MODEL_WIDTH:].reshape(head_shape)
    attn_mix = attention_rows(queries, keys_all, values_all, seg_rows).reshape(row_count, row_len, MODEL_WIDTH)
    attn_mix = low(low_back(attn_mix))
    attn_out = low_back(jnp.einsum('rld,de->rle', attn_mix, mat_out, precision=highest) + bias_out)
    resid_one = row_vals + attn_out
    hidden_two = low(layer_norm(resid_one, gain_two, shift_two))
    up_pre = low_back(jnp.einsum('rld,de->rle', hidden_two, mat_up, precision=highest) + bias_up)
    act_low = low(gelu_tanh(up_pre))
    down_out = low_back(jnp.einsum('rle,ed->rld', act_low, mat_down, precision=highest) + bias_down)
    return resid_one + down_out

def forward(params, token_vals, segment_ids):
    mat_qkv, mat_out, mat_up, mat_down, vector_all = params
    weights = (low(mat_qkv), low(mat_out), low(mat_up), low(mat_down)) + split_small(low(vector_all))
    row_count, row_len = (token_vals.shape[0], token_vals.shape[1])
    batch_rows = math.gcd(row_count, max(1, 4096 // row_len))
    batch_count = row_count // batch_rows
    checked_block = jax.checkpoint(block_rows)
    block_outs = lax.map(lambda batch_pair: checked_block(weights, batch_pair[0], batch_pair[1]), (token_vals.reshape(batch_count, batch_rows, row_len, MODEL_WIDTH), segment_ids.reshape(batch_count, batch_rows, row_len)))
    return block_outs.reshape(row_count, row_len, MODEL_WIDTH)

def adamw_update(weight, gradient, first_mom, second, step_rate, decay_rate):
    first_new = beta_one * first_mom + (1.0 - beta_one) * gradient
    second_new = beta_two * second + (1.0 - beta_two) * gradient * gradient
    first_hat = first_new / (1.0 - beta_one ** STEP)
    second_hat = second_new / (1.0 - beta_two ** STEP)
    weight_new = weight - step_rate * (first_hat / (jnp.sqrt(second_hat) + adam_eps) + decay_rate * weight)
    return (weight_new, first_new, second_new)

def reference(tokens, output_gradient, segment_ids, row_fill, w_qkv, w_attn_out, w_up, w_down, vectors, momentum_qkv_weight, momentum_attn_output, momentum_up_weight, momentum_down_weight, momentum_vector_rows, second_qkv, second_attn_out, second_up, second_down, second_vectors):
    params = (w_qkv, w_attn_out, w_up, w_down, vectors)
    inputs_f = tokens.astype(jnp.float32)
    block_outs, pull_back = jax.vjp(lambda param_set, token_vals: forward(param_set, token_vals, segment_ids), params, inputs_f)
    slot_numbers = jnp.arange(PACKED_LENGTH, dtype=jnp.int32)
    live_mask = (slot_numbers[None, :] < row_fill[:, None]).astype(jnp.float32)
    cotangent = output_gradient.astype(jnp.float32) * live_mask[:, :, None]
    param_grads, input_grad = pull_back(cotangent)
    grad_qkv, grad_out, grad_up, grad_down, grad_vec = param_grads
    new_qkv, mom_qkv, sec_qkv = adamw_update(w_qkv, grad_qkv, momentum_qkv_weight, second_qkv, 0.05, 0.1)
    new_out, mom_out, sec_out = adamw_update(w_attn_out, grad_out, momentum_attn_output, second_attn_out, 0.05, 0.1)
    new_up, mom_up, sec_up = adamw_update(w_up, grad_up, momentum_up_weight, second_up, 0.05, 0.1)
    new_down, mom_down, sec_down = adamw_update(w_down, grad_down, momentum_down_weight, second_down, 0.05, 0.1)
    new_vec, mom_vec, sec_vec = adamw_update(vectors, grad_vec, momentum_vector_rows, second_vectors, 0.6, 0.0)
    return (block_outs.astype(jnp.bfloat16), input_grad, new_qkv, new_out, new_up, new_down, new_vec, mom_qkv, mom_out, mom_up, mom_down, mom_vec, sec_qkv, sec_out, sec_up, sec_down, sec_vec)
```

```python
import jax
import jax.numpy as jnp
from jax import lax
from jax.sharding import PartitionSpec as P

MODEL_WIDTH = 1024
HEADS = 16
HEAD_DIM = 64
HIDDEN_UNITS = 4096
STEP = 10


norm_eps = 1e-05
score_scale = 0.125
masked_score = -1e30
gelu_coef = 0.7978845608028654
beta_one = 0.9
beta_two = 0.95
adam_eps = 1e-08


def layer_norm(inputs, scale_vec, shift_vec):
    centre = inputs - jnp.mean(inputs, axis=-1, keepdims=True)
    spread = jnp.mean(centre * centre, axis=-1, keepdims=True)
    return centre * lax.rsqrt(spread + norm_eps) * scale_vec + shift_vec


def gelu_tanh(points):
    return (
        0.5 * points * (1.0 + jnp.tanh(gelu_coef * (points + 0.044715 * points * points * points)))
    )


def alibi_slopes(count_heads):
    return jnp.power(2.0, -8.0 * (jnp.arange(count_heads, dtype=jnp.float32) + 1.0) / count_heads)


def split_small(vector_all):
    bounds = [
        0,
        MODEL_WIDTH,
        2 * MODEL_WIDTH,
        5 * MODEL_WIDTH,
        6 * MODEL_WIDTH,
        7 * MODEL_WIDTH,
        8 * MODEL_WIDTH,
        8 * MODEL_WIDTH + HIDDEN_UNITS,
        9 * MODEL_WIDTH + HIDDEN_UNITS,
    ]
    return tuple(
        (vector_all[low_end:high_end] for low_end, high_end in zip(bounds[:-1], bounds[1:]))
    )


def outer_sum(left_mat, right_mat):
    return lax.dot_general(
        left_mat, right_mat, (((0,), (0,)), ((), ())), preferred_element_type=jnp.float32
    )


def times_trans(left_mat, right_mat):
    return lax.dot_general(
        left_mat, right_mat, (((1,), (1,)), ((), ())), preferred_element_type=jnp.float32
    )


def adamw_update(weight, gradient, first_mom, second, step_rate, decay_rate):
    first_new = beta_one * first_mom + (1.0 - beta_one) * gradient
    second_new = beta_two * second + (1.0 - beta_two) * gradient * gradient
    first_hat = first_new / (1.0 - beta_one**STEP)
    second_hat = second_new / (1.0 - beta_two**STEP)
    weight_new = weight - step_rate * (
        first_hat / (jnp.sqrt(second_hat) + adam_eps) + decay_rate * weight
    )
    return (weight_new, first_new, second_new)


def shards(
    tokens,
    output_gradient,
    segment_ids,
    row_fill,
    w_qkv,
    w_attn_out,
    w_up,
    w_down,
    vectors,
    momentum_qkv_weight,
    momentum_attn_output,
    momentum_up_weight,
    momentum_down_weight,
    momentum_vector_rows,
    second_qkv,
    second_attn_out,
    second_up,
    second_down,
    second_vectors,
):
    parts, group = lax.axis_size("ctx"), lax.axis_size("fsdp")
    own = lax.axis_index("ctx")
    block = MODEL_WIDTH // parts
    hid = HIDDEN_UNITS // parts
    heads = HEADS // parts
    rows_in, rows_out, vec_len = w_qkv.shape[0], w_attn_out.shape[0], vectors.shape[0]
    tall = parts * rows_in
    folds = tall // rows_out
    fold_wide = MODEL_WIDTH // folds
    wide_qkv = 3 * block
    tokens_loc, grads_loc = tokens[0], output_gradient[0]
    length = tokens_loc.shape[0]
    seg_row = segment_ids[0]
    full_len = seg_row.shape[0]
    place_all = jnp.arange(full_len, dtype=jnp.int32)
    live_all = place_all < row_fill[0]
    place_loc = own * length + jnp.arange(length, dtype=jnp.int32)
    live_loc = place_loc < row_fill[0]

    vec_pad = jnp.pad(vectors.astype(jnp.bfloat16)[None, :], ((0, 15), (0, MODEL_WIDTH - vec_len)))
    seq_pack = lax.all_gather(
        jnp.concatenate([tokens_loc, grads_loc, vec_pad], axis=0), "ctx", axis=0, tiled=False
    )
    rows_all = seq_pack[:, :length].reshape(full_len, MODEL_WIDTH).astype(jnp.float32)
    dy_all = seq_pack[:, length : 2 * length].reshape(full_len, MODEL_WIDTH)
    dy_all = jnp.where(live_all[:, None], dy_all, jnp.zeros_like(dy_all))
    vec_ctx = seq_pack[:, 2 * length]

    send = jnp.concatenate(
        [
            w_qkv.astype(jnp.bfloat16)
            .reshape(rows_in, 3, parts, block)
            .transpose(2, 0, 1, 3)
            .reshape(parts, rows_in, wide_qkv),
            w_up.astype(jnp.bfloat16).reshape(rows_in, parts, hid).transpose(1, 0, 2),
        ],
        axis=2,
    )
    cols = lax.all_to_all(send, "ctx", 0, 0).reshape(tall, wide_qkv + hid)
    low_out = w_attn_out.astype(jnp.bfloat16)
    out_fold = jnp.concatenate(
        [low_out[:, i * fold_wide : (i + 1) * fold_wide] for i in range(folds)], axis=0
    )
    wide = wide_qkv + hid + MODEL_WIDTH + fold_wide
    pack = jnp.concatenate([cols, w_down.astype(jnp.bfloat16), out_fold], axis=1)
    vec_rows = jnp.pad(vec_ctx, ((0, 16 - parts), (0, wide - MODEL_WIDTH)))
    full = lax.all_gather(jnp.concatenate([pack, vec_rows], axis=0), "fsdp", axis=0, tiled=False)
    mats = full[:, :tall]

    def columns_whole(part):
        return (
            part.reshape(group, parts, rows_in, -1)
            .transpose(1, 0, 2, 3)
            .reshape(parts * group * rows_in, -1)
        )

    mat_qkv = columns_whole(mats[:, :, :wide_qkv])
    mat_up = columns_whole(mats[:, :, wide_qkv : wide_qkv + hid])
    mat_down = mats[:, :, wide_qkv + hid : wide_qkv + hid + MODEL_WIDTH].reshape(hid, MODEL_WIDTH)
    mat_out = (
        mats[:, :, wide_qkv + hid + MODEL_WIDTH :]
        .reshape(group, folds, rows_out, fold_wide)
        .transpose(0, 2, 1, 3)
        .reshape(block, MODEL_WIDTH)
    )
    vec_full = full[:, tall : tall + parts, :vec_len].transpose(1, 0, 2).reshape(-1)
    gain_one, shift_one, bias_qkv, bias_out, gain_two, shift_two, bias_up, bias_down = split_small(
        vec_full.astype(jnp.float32)
    )
    bias_qkv_own = lax.dynamic_slice_in_dim(
        bias_qkv.reshape(3, MODEL_WIDTH), own * block, block, axis=1
    ).reshape(-1)
    bias_up_own = lax.dynamic_slice_in_dim(bias_up, own * hid, hid)

    normed_one = layer_norm(rows_all, gain_one, shift_one)
    hidden_one = normed_one.astype(jnp.bfloat16)
    qkv_low = (
        jnp.dot(hidden_one, mat_qkv, preferred_element_type=jnp.float32) + bias_qkv_own
    ).astype(jnp.bfloat16)
    heads_q = qkv_low[:, :block].reshape(full_len, heads, HEAD_DIM)
    heads_k = qkv_low[:, block : 2 * block].reshape(full_len, heads, HEAD_DIM)
    heads_v = qkv_low[:, 2 * block :].reshape(full_len, heads, HEAD_DIM)
    allowed = (place_all[None, :] <= place_all[:, None]) & (seg_row[:, None] == seg_row[None, :])
    distance = (place_all[:, None] - place_all[None, :]).astype(jnp.float32)
    slopes = lax.dynamic_slice_in_dim(alibi_slopes(HEADS), own * heads, heads)
    scores = (
        jnp.einsum("qhd,khd->hqk", heads_q, heads_k, preferred_element_type=jnp.float32)
        * score_scale
        - slopes[:, None, None] * distance[None]
    )
    scores = jnp.where(allowed[None], scores, masked_score)
    row_max = jnp.max(scores, axis=-1, keepdims=True)
    exp_scores = jnp.exp(scores - row_max)
    probs_vals = exp_scores / jnp.sum(exp_scores, axis=-1, keepdims=True)
    probs_low = probs_vals.astype(jnp.bfloat16)
    attn_mix = jnp.einsum("hqk,khd->qhd", probs_low, heads_v, preferred_element_type=jnp.float32)
    attn_mix = attn_mix.reshape(full_len, block).astype(jnp.bfloat16)
    attn_part = jnp.dot(attn_mix, mat_out, preferred_element_type=jnp.float32)
    attn_out = lax.psum_scatter(
        attn_part.astype(jnp.bfloat16), "ctx", scatter_dimension=0, tiled=True
    )
    rows_loc = tokens_loc.astype(jnp.float32)
    resid_one = rows_loc + (attn_out.astype(jnp.float32) + bias_out)

    normed_two, ln_two_pull = jax.vjp(layer_norm, resid_one, gain_two, shift_two)
    hidden_two = lax.all_gather(normed_two.astype(jnp.bfloat16), "ctx", axis=0, tiled=True)
    up_pre = jnp.dot(hidden_two, mat_up, preferred_element_type=jnp.float32) + bias_up_own
    act_out, gelu_pull = jax.vjp(gelu_tanh, up_pre)
    act_low = act_out.astype(jnp.bfloat16)
    grad_act = times_trans(dy_all, mat_down)
    grad_up_low = gelu_pull(grad_act)[0].astype(jnp.bfloat16)
    grad_normed_part = times_trans(grad_up_low, mat_up).astype(jnp.bfloat16)
    grad_normed_two = lax.psum_scatter(grad_normed_part, "ctx", scatter_dimension=0, tiled=True)
    dy_loc = jnp.where(live_loc[:, None], grads_loc, jnp.zeros_like(grads_loc)).astype(jnp.float32)
    grad_bias_down = jnp.sum(dy_loc, axis=0)
    grad_bias_up = jnp.sum(grad_up_low.astype(jnp.float32), axis=0)
    grad_resid_ln, grad_gain_two, grad_shift_two = ln_two_pull(grad_normed_two.astype(jnp.float32))
    grad_resid = dy_loc + grad_resid_ln
    grad_attn_loc = grad_resid.astype(jnp.bfloat16)
    grad_bias_out = jnp.sum(grad_attn_loc.astype(jnp.float32), axis=0)
    grad_attn = lax.all_gather(grad_attn_loc, "ctx", axis=0, tiled=True)

    down_part = jnp.dot(act_low, mat_down, preferred_element_type=jnp.float32).astype(jnp.bfloat16)
    ffn_pack = jnp.concatenate(
        [
            outer_sum(hidden_two, grad_up_low)
            .reshape(parts, group, rows_in, hid)
            .transpose(1, 0, 2, 3)
            .reshape(group, tall, hid),
            outer_sum(act_low, dy_all).reshape(group, tall, MODEL_WIDTH),
        ],
        axis=2,
    ).astype(jnp.bfloat16)
    grad_attn, down_part, ffn_pack = lax.optimization_barrier((grad_attn, down_part, ffn_pack))
    down_out = lax.psum_scatter(down_part, "ctx", scatter_dimension=0, tiled=True)
    block_out = (resid_one + (down_out.astype(jnp.float32) + bias_down)).astype(jnp.bfloat16)[None]
    ffn_sum = lax.psum_scatter(
        ffn_pack.reshape(group * tall, -1), "fsdp", scatter_dimension=0, tiled=True
    )

    grad_mixed = times_trans(grad_attn, mat_out).astype(jnp.bfloat16)
    grad_mixed = grad_mixed.reshape(full_len, heads, HEAD_DIM)
    grad_value = jnp.einsum(
        "hqk,qhd->khd", probs_low, grad_mixed, preferred_element_type=jnp.float32
    )
    grad_probs = jnp.einsum("qhd,khd->hqk", grad_mixed, heads_v, preferred_element_type=jnp.float32)
    grad_scores = probs_vals * (
        grad_probs - jnp.sum(probs_vals * grad_probs, axis=-1, keepdims=True)
    )
    grad_scores_low = grad_scores.astype(jnp.bfloat16)
    grad_query = (
        jnp.einsum("hqk,khd->qhd", grad_scores_low, heads_k, preferred_element_type=jnp.float32)
        * score_scale
    )
    grad_key = (
        jnp.einsum("hqk,qhd->khd", grad_scores_low, heads_q, preferred_element_type=jnp.float32)
        * score_scale
    )
    grad_qkv_low = jnp.concatenate(
        [part.reshape(full_len, block) for part in (grad_query, grad_key, grad_value)], axis=1
    ).astype(jnp.bfloat16)
    grad_bias_qkv = jnp.sum(grad_qkv_low.astype(jnp.float32), axis=0)
    grad_first_part = times_trans(grad_qkv_low, mat_qkv).astype(jnp.bfloat16)
    grad_normed_one = lax.psum_scatter(grad_first_part, "ctx", scatter_dimension=0, tiled=True)
    _, ln_one_pull = jax.vjp(layer_norm, rows_loc, gain_one, shift_one)
    grad_rows_ln, grad_gain_one, grad_shift_one = ln_one_pull(grad_normed_one.astype(jnp.float32))
    tokens_grad = (grad_resid + grad_rows_ln)[None]

    def own_columns(values, count):
        wide_all = jnp.zeros((count, parts, values.size // count), jnp.float32)
        return lax.dynamic_update_slice(
            wide_all, values.reshape(count, 1, -1), (0, own, 0)
        ).reshape(-1)

    grad_vec = jnp.concatenate(
        [
            grad_gain_one,
            grad_shift_one,
            own_columns(grad_bias_qkv, 3),
            grad_bias_out,
            grad_gain_two,
            grad_shift_two,
            own_columns(grad_bias_up, 1),
            grad_bias_down,
        ]
    )
    attn_wide = wide_qkv + fold_wide
    attn_pack = jnp.concatenate(
        [
            outer_sum(hidden_one, grad_qkv_low)
            .reshape(parts, group, rows_in, wide_qkv)
            .transpose(1, 0, 2, 3)
            .reshape(group, tall, wide_qkv),
            outer_sum(attn_mix, grad_attn)
            .reshape(group, rows_out, folds, fold_wide)
            .transpose(0, 2, 1, 3)
            .reshape(group, tall, fold_wide),
        ],
        axis=2,
    )
    vec_pack = jnp.pad(
        grad_vec.reshape(parts, group, vec_len).transpose(1, 0, 2),
        ((0, 0), (0, 16 - parts), (0, attn_wide - vec_len)),
    )
    attn_pack = jnp.concatenate([attn_pack, vec_pack], axis=1).astype(jnp.bfloat16)
    attn_sum = lax.psum_scatter(
        attn_pack.reshape(group * (tall + 16), attn_wide), "fsdp", scatter_dimension=0, tiled=True
    )

    total_ffn = lax.psum(ffn_sum, "replica")
    ffn_cols = lax.all_to_all(total_ffn[:, :hid].reshape(parts, rows_in, hid), "ctx", 0, 0)
    total_up = ffn_cols.transpose(1, 0, 2).reshape(w_up.shape).astype(jnp.float32)
    total_down = total_ffn[:, hid:].astype(jnp.float32)
    total_attn = lax.psum(attn_sum, "replica")
    total_out = (
        total_attn[:tall, wide_qkv:]
        .reshape(folds, rows_out, fold_wide)
        .transpose(1, 0, 2)
        .reshape(w_attn_out.shape)
        .astype(jnp.float32)
    )
    vec_send = jnp.pad(
        total_attn[tall : tall + parts, :vec_len], ((0, 0), (0, 2 * wide_qkv - vec_len))
    ).reshape(parts, 2, wide_qkv)
    qkv_cols = lax.all_to_all(
        jnp.concatenate(
            [
                total_attn[:tall, :wide_qkv].reshape(parts, rows_in, wide_qkv),
                jnp.pad(vec_send, ((0, 0), (0, 14), (0, 0))),
            ],
            axis=1,
        ),
        "ctx",
        0,
        0,
    )
    total_qkv = (
        qkv_cols[:, :rows_in]
        .reshape(parts, rows_in, 3, block)
        .transpose(1, 2, 0, 3)
        .reshape(w_qkv.shape)
        .astype(jnp.float32)
    )
    total_vec = jnp.sum(
        qkv_cols[:, rows_in : rows_in + 2].astype(jnp.float32), axis=0
    ).reshape(-1)[:vec_len]
    new_qkv, mom_qkv, sec_qkv = adamw_update(
        w_qkv, total_qkv, momentum_qkv_weight, second_qkv, 0.05, 0.1
    )
    new_out, mom_out, sec_out = adamw_update(
        w_attn_out, total_out, momentum_attn_output, second_attn_out, 0.05, 0.1
    )
    new_up, mom_up, sec_up = adamw_update(w_up, total_up, momentum_up_weight, second_up, 0.05, 0.1)
    new_down, mom_down, sec_down = adamw_update(
        w_down, total_down, momentum_down_weight, second_down, 0.05, 0.1
    )
    new_vec, mom_vec, sec_vec = adamw_update(
        vectors, total_vec, momentum_vector_rows, second_vectors, 0.6, 0.0
    )
    return (
        block_out,
        tokens_grad,
        new_qkv,
        new_out,
        new_up,
        new_down,
        new_vec,
        mom_qkv,
        mom_out,
        mom_up,
        mom_down,
        mom_vec,
        sec_qkv,
        sec_out,
        sec_up,
        sec_down,
        sec_vec,
    )


def solution(mesh):
    placed = (
        P(("fsdp", "replica"), "ctx", None),
        P(("fsdp", "replica"), "ctx", None),
        P(("fsdp", "replica"), None),
        P(("fsdp", "replica")),
        P(("ctx", "fsdp"), None),
        P(("ctx", "fsdp"), None),
        P(("ctx", "fsdp"), None),
        P(("ctx", "fsdp"), None),
        P(("ctx", "fsdp")),
        P(("ctx", "fsdp"), None),
        P(("ctx", "fsdp"), None),
        P(("ctx", "fsdp"), None),
        P(("ctx", "fsdp"), None),
        P(("ctx", "fsdp")),
        P(("ctx", "fsdp"), None),
        P(("ctx", "fsdp"), None),
        P(("ctx", "fsdp"), None),
        P(("ctx", "fsdp"), None),
        P(("ctx", "fsdp")),
    )
    return jax.shard_map(
        shards,
        mesh=mesh,
        in_specs=placed,
        out_specs=(
            P(("fsdp", "replica"), "ctx", None),
            P(("fsdp", "replica"), "ctx", None),
            P(("ctx", "fsdp"), None),
            P(("ctx", "fsdp"), None),
            P(("ctx", "fsdp"), None),
            P(("ctx", "fsdp"), None),
            P(("ctx", "fsdp")),
            P(("ctx", "fsdp"), None),
            P(("ctx", "fsdp"), None),
            P(("ctx", "fsdp"), None),
            P(("ctx", "fsdp"), None),
            P(("ctx", "fsdp")),
            P(("ctx", "fsdp"), None),
            P(("ctx", "fsdp"), None),
            P(("ctx", "fsdp"), None),
            P(("ctx", "fsdp"), None),
            P(("ctx", "fsdp")),
        ),
        check_vma=False,
    )
```

```python
import functools

import jax
import jax.numpy as jnp
from jax import lax
from jax.experimental import pallas as pl
from jax.experimental.pallas import tpu as pltpu
from jax.sharding import PartitionSpec as P

MODEL_WIDTH = 1024
HEADS = 16
HEAD_DIM = 64
HIDDEN_UNITS = 4096
STEP = 10

MESH = pl.DeviceIdType.MESH


norm_eps = 1e-05
score_scale = 0.125
masked_score = -1e30
gelu_coef = 0.7978845608028654
beta_one = 0.9
beta_two = 0.95
adam_eps = 1e-08


def layer_norm(inputs, scale_vec, shift_vec):
    centre = inputs - jnp.mean(inputs, axis=-1, keepdims=True)
    spread = jnp.mean(centre * centre, axis=-1, keepdims=True)
    return centre * lax.rsqrt(spread + norm_eps) * scale_vec + shift_vec


def gelu_tanh(points):
    return (
        0.5 * points * (1.0 + jnp.tanh(gelu_coef * (points + 0.044715 * points * points * points)))
    )


def alibi_slopes(count_heads):
    return jnp.power(2.0, -8.0 * (jnp.arange(count_heads, dtype=jnp.float32) + 1.0) / count_heads)


def split_small(vector_all):
    bounds = [
        0,
        MODEL_WIDTH,
        2 * MODEL_WIDTH,
        5 * MODEL_WIDTH,
        6 * MODEL_WIDTH,
        7 * MODEL_WIDTH,
        8 * MODEL_WIDTH,
        8 * MODEL_WIDTH + HIDDEN_UNITS,
        9 * MODEL_WIDTH + HIDDEN_UNITS,
    ]
    return tuple(
        (vector_all[low_end:high_end] for low_end, high_end in zip(bounds[:-1], bounds[1:]))
    )


def outer_sum(left_mat, right_mat):
    return lax.dot_general(
        left_mat, right_mat, (((0,), (0,)), ((), ())), preferred_element_type=jnp.float32
    )


def times_trans(left_mat, right_mat):
    return lax.dot_general(
        left_mat, right_mat, (((1,), (1,)), ((), ())), preferred_element_type=jnp.float32
    )


def adamw_update(weight, gradient, first_mom, second, step_rate, decay_rate):
    first_new = beta_one * first_mom + (1.0 - beta_one) * gradient
    second_new = beta_two * second + (1.0 - beta_two) * gradient * gradient
    first_hat = first_new / (1.0 - beta_one**STEP)
    second_hat = second_new / (1.0 - beta_two**STEP)
    weight_new = weight - step_rate * (
        first_hat / (jnp.sqrt(second_hat) + adam_eps) + decay_rate * weight
    )
    return (weight_new, first_new, second_new)


def enter(group, me_f, me_r):
    barrier = pltpu.get_barrier_semaphore()
    for step in range(1, group):
        pl.semaphore_signal(
            barrier, inc=1, device_id={"fsdp": lax.rem(me_f + step, group)}, device_id_type=MESH
        )
    pl.semaphore_signal(barrier, inc=1, device_id={"replica": 1 - me_r}, device_id_type=MESH)
    pl.semaphore_wait(barrier, group)


def gather_kernel(group, kinds, *refs):
    count = len(kinds)
    ins, outs = refs[:count], refs[count : 2 * count]
    local_sem, send_sem, recv_sem, pass_send, pass_recv = refs[2 * count :]
    me_f, me_r = lax.axis_index("fsdp"), lax.axis_index("replica")
    enter(group, me_f, me_r)

    def spot(index, owner, half):
        if kinds[index]:
            return outs[index].at[half, owner]
        return outs[index].at[owner, half]

    halves, waits = [], []
    for index in range(count):
        size = ins[index].shape[0] // 2
        halves.append(pl.ds(me_r * size, size))
    for index in range(count):
        for step in range(1, group):
            copy = pltpu.make_async_remote_copy(
                src_ref=ins[index].at[halves[index]],
                dst_ref=spot(index, me_f, halves[index]),
                send_sem=send_sem.at[index, step - 1],
                recv_sem=recv_sem.at[index, step - 1],
                device_id={"fsdp": lax.rem(me_f + step, group)},
                device_id_type=MESH,
            )
            copy.start()
            waits.append((copy, index, step))
    own = []
    for index in range(count):
        whole = pl.ds(0, ins[index].shape[0])
        copy = pltpu.make_async_copy(ins[index], spot(index, me_f, whole), local_sem.at[index])
        copy.start()
        own.append(copy)
    passed = []
    for copy, index, step in waits:
        copy.wait_recv()
        sender = lax.rem(me_f + group - step, group)
        part = spot(index, sender, halves[index])
        onward = pltpu.make_async_remote_copy(
            src_ref=part,
            dst_ref=part,
            send_sem=pass_send.at[index, step - 1],
            recv_sem=pass_recv.at[index, step - 1],
            device_id={"replica": 1 - me_r},
            device_id_type=MESH,
        )
        onward.start()
        passed.append(onward)
    for copy, _, _ in waits:
        copy.wait_send()
    for copy in own:
        copy.wait()
    for copy in passed:
        copy.wait()


def gather_over_group(arrays, kinds, group):
    shapes = [
        (item.shape[0], group) + item.shape[1:] if kind else (group,) + item.shape
        for item, kind in zip(arrays, kinds)
    ]
    count = len(arrays)
    return pl.pallas_call(
        functools.partial(gather_kernel, group, kinds),
        out_shape=[
            jax.ShapeDtypeStruct(shape, item.dtype) for shape, item in zip(shapes, arrays)
        ],
        in_specs=[pl.BlockSpec(memory_space=pl.ANY)] * count,
        out_specs=[pl.BlockSpec(memory_space=pl.ANY)] * count,
        scratch_shapes=[pltpu.SemaphoreType.DMA((count,))]
        + [pltpu.SemaphoreType.DMA((count, group - 1))] * 4,
        compiler_params=pltpu.CompilerParams(collective_id=0, has_side_effects=True),
        cost_estimate=pl.CostEstimate(flops=0, bytes_accessed=120_000_000, transcendentals=0),
    )(*arrays)


def reduce_kernel(group, kinds, *refs):
    count = len(kinds)
    ins, outs = refs[:count], refs[count : 2 * count]
    firsts, seconds = refs[2 * count : 3 * count], refs[3 * count : 4 * count]
    core_send, core_recv, send_sem, recv_sem, pass_send, pass_recv = refs[4 * count :]
    me_f, me_r = lax.axis_index("fsdp"), lax.axis_index("replica")
    enter(group, me_f, me_r)
    sizes = [out.shape[0] // 2 for out in outs]

    def core_copy(source, target, sends, recvs, index):
        return pltpu.make_async_remote_copy(
            src_ref=source,
            dst_ref=target,
            send_sem=sends.at[index],
            recv_sem=recvs.at[index],
            device_id={"replica": 1 - me_r},
            device_id_type=MESH,
        )

    def at(ref, index, half, owner):
        return ref.at[half, owner] if kinds[index] else ref.at[owner, half]

    every = pl.ds(0, group)
    first_copies = []
    for index in range(count):
        other = pl.ds((1 - me_r) * sizes[index], sizes[index])
        copy = core_copy(
            at(ins[index], index, other, every), firsts[index], core_send, core_recv, index
        )
        copy.start()
        first_copies.append(copy)
    peer_copies = []
    for index in range(count):
        first_copies[index].wait_recv()
        for step in list(range(1, group)) + [0]:
            owner = lax.rem(me_f + step, group)

            def add(place, carry, index=index, owner=owner):
                here = at(firsts[index], index, place, owner)
                mine = at(ins[index], index, me_r * sizes[index] + place, owner)
                here[...] = (
                    here[...].astype(jnp.float32) + mine[...].astype(jnp.float32)
                ).astype(here.dtype)
                return carry

            lax.fori_loop(0, sizes[index], add, 0)
            if step:
                copy = pltpu.make_async_remote_copy(
                    src_ref=at(firsts[index], index, pl.ds(0, sizes[index]), owner),
                    dst_ref=seconds[index].at[step - 1],
                    send_sem=send_sem.at[index, step - 1],
                    recv_sem=recv_sem.at[index, step - 1],
                    device_id={"fsdp": owner},
                    device_id_type=MESH,
                )
                copy.start()
                peer_copies.append(copy)
    last_copies = []
    for index in range(count):
        for step in range(1, group):
            peer_copies[index * (group - 1) + step - 1].wait_recv()

        def total(place, carry, index=index):
            value = at(firsts[index], index, place, me_f)[...].astype(jnp.float32)
            for step in range(1, group):
                value += seconds[index][step - 1, place].astype(jnp.float32)
            outs[index][me_r * sizes[index] + place] = value.astype(outs[index].dtype)
            return carry

        lax.fori_loop(0, sizes[index], total, 0)
        part = outs[index].at[pl.ds(me_r * sizes[index], sizes[index])]
        copy = core_copy(part, part, pass_send, pass_recv, index)
        copy.start()
        last_copies.append(copy)
    for copy in first_copies + peer_copies:
        copy.wait_send()
    for copy in last_copies:
        copy.wait()


def reduce_over_group(arrays, kinds, group, name):
    count = len(arrays)
    outs, firsts, seconds = [], [], []
    for item, kind in zip(arrays, kinds):
        lead = item.shape[0] if kind else item.shape[1]
        rest = item.shape[2:]
        outs.append((lead,) + rest)
        half = lead // 2
        firsts.append(((half, group) if kind else (group, half)) + rest)
        seconds.append((group - 1, half) + rest)
    return pl.pallas_call(
        functools.partial(reduce_kernel, group, kinds),
        out_shape=[
            jax.ShapeDtypeStruct(shape, item.dtype) for shape, item in zip(outs, arrays)
        ],
        in_specs=[pl.BlockSpec(memory_space=pltpu.VMEM)] * count,
        out_specs=[pl.BlockSpec(memory_space=pltpu.VMEM)] * count,
        scratch_shapes=[
            pltpu.VMEM(shape, item.dtype) for shape, item in zip(firsts + seconds, arrays + arrays)
        ]
        + [pltpu.SemaphoreType.DMA((count,))] * 2
        + [pltpu.SemaphoreType.DMA((count, group - 1))] * 2
        + [pltpu.SemaphoreType.DMA((count,))] * 2,
        compiler_params=pltpu.CompilerParams(
            collective_id=name, has_side_effects=True, vmem_limit_bytes=24 * 1024 * 1024
        ),
        cost_estimate=pl.CostEstimate(flops=0, bytes_accessed=100_000_000, transcendentals=0),
    )(*arrays)


def plain_gather(arrays, kinds, group):
    return [
        lax.all_gather(item, "fsdp", axis=1 if kind else 0, tiled=False)
        for item, kind in zip(arrays, kinds)
    ]


def plain_reduce(arrays, kinds, group, name):
    return [
        lax.psum(lax.psum_scatter(item, "fsdp", scatter_dimension=1 if kind else 0), "replica")
        for item, kind in zip(arrays, kinds)
    ]


def shards(
    tokens,
    output_gradient,
    segment_ids,
    row_fill,
    w_qkv,
    w_attn_out,
    w_up,
    w_down,
    vectors,
    momentum_qkv_weight,
    momentum_attn_output,
    momentum_up_weight,
    momentum_down_weight,
    momentum_vector_rows,
    second_qkv,
    second_attn_out,
    second_up,
    second_down,
    second_vectors,
):
    parts, group = lax.axis_size("ctx"), lax.axis_size("fsdp")
    own = lax.axis_index("ctx")
    block = MODEL_WIDTH // parts
    hid = HIDDEN_UNITS // parts
    heads = HEADS // parts
    rows_in, rows_out, vec_len = w_qkv.shape[0], w_attn_out.shape[0], vectors.shape[0]
    paired = lax.axis_size("replica") == 2
    gather_all = gather_over_group if paired else plain_gather
    reduce_all = reduce_over_group if paired else plain_reduce
    wide_qkv = 3 * block
    tokens_loc, grads_loc = tokens[0], output_gradient[0]
    length = tokens_loc.shape[0]
    seg_row = segment_ids[0]
    full_len = seg_row.shape[0]
    place_all = jnp.arange(full_len, dtype=jnp.int32)
    live_all = place_all < row_fill[0]
    place_loc = own * length + jnp.arange(length, dtype=jnp.int32)
    live_loc = place_loc < row_fill[0]

    rows_all = lax.all_gather(tokens_loc, "ctx", axis=0, tiled=True).astype(jnp.float32)
    dy_all = lax.all_gather(grads_loc, "ctx", axis=0, tiled=True)
    dy_all = jnp.where(live_all[:, None], dy_all, jnp.zeros_like(dy_all))

    vec_tile = jnp.pad(vectors.astype(jnp.bfloat16), (0, 2048 - vec_len)).reshape(16, 128)
    vec_tile = jnp.pad(vec_tile, ((0, 0), (0, wide_qkv + hid - 128)))
    send = jnp.concatenate(
        [
            w_qkv.astype(jnp.bfloat16)
            .reshape(rows_in, 3, parts, block)
            .transpose(2, 0, 1, 3)
            .reshape(parts, rows_in, wide_qkv),
            w_up.astype(jnp.bfloat16).reshape(rows_in, parts, hid).transpose(1, 0, 2),
        ],
        axis=2,
    )
    send = jnp.concatenate(
        [send, jnp.broadcast_to(vec_tile[None], (parts,) + vec_tile.shape)], axis=1
    )
    cols = lax.all_to_all(send, "ctx", 0, 0)
    mat_qkv, mat_out, mat_up, mat_down, vec_full = gather_all(
        [
            cols[:, :rows_in, :wide_qkv],
            w_attn_out.astype(jnp.bfloat16).reshape(2, rows_out // 2, MODEL_WIDTH),
            cols[:, :rows_in, wide_qkv:],
            w_down.astype(jnp.bfloat16).reshape(parts, -1, MODEL_WIDTH),
            cols[:, rows_in:, :128],
        ],
        (True, False, True, False, True),
        group,
    )
    mat_qkv = mat_qkv.reshape(MODEL_WIDTH, wide_qkv)
    mat_up = mat_up.reshape(MODEL_WIDTH, hid)
    mat_down = mat_down.reshape(hid, MODEL_WIDTH)
    mat_out = mat_out.reshape(block, MODEL_WIDTH)
    vec_full = vec_full.reshape(parts * group, 2048)[:, :vec_len].reshape(-1)
    gain_one, shift_one, bias_qkv, bias_out, gain_two, shift_two, bias_up, bias_down = split_small(
        vec_full.astype(jnp.float32)
    )
    bias_qkv_own = lax.dynamic_slice_in_dim(
        bias_qkv.reshape(3, MODEL_WIDTH), own * block, block, axis=1
    ).reshape(-1)
    bias_up_own = lax.dynamic_slice_in_dim(bias_up, own * hid, hid)

    normed_one = layer_norm(rows_all, gain_one, shift_one)
    hidden_one = normed_one.astype(jnp.bfloat16)
    qkv_low = (
        jnp.dot(hidden_one, mat_qkv, preferred_element_type=jnp.float32) + bias_qkv_own
    ).astype(jnp.bfloat16)
    heads_q = qkv_low[:, :block].reshape(full_len, heads, HEAD_DIM)
    heads_k = qkv_low[:, block : 2 * block].reshape(full_len, heads, HEAD_DIM)
    heads_v = qkv_low[:, 2 * block :].reshape(full_len, heads, HEAD_DIM)
    allowed = (place_all[None, :] <= place_all[:, None]) & (seg_row[:, None] == seg_row[None, :])
    distance = (place_all[:, None] - place_all[None, :]).astype(jnp.float32)
    slopes = lax.dynamic_slice_in_dim(alibi_slopes(HEADS), own * heads, heads)
    scores = (
        jnp.einsum("qhd,khd->hqk", heads_q, heads_k, preferred_element_type=jnp.float32)
        * score_scale
        - slopes[:, None, None] * distance[None]
    )
    scores = jnp.where(allowed[None], scores, masked_score)
    row_max = jnp.max(scores, axis=-1, keepdims=True)
    exp_scores = jnp.exp(scores - row_max)
    probs_vals = exp_scores / jnp.sum(exp_scores, axis=-1, keepdims=True)
    probs_low = probs_vals.astype(jnp.bfloat16)
    attn_mix = jnp.einsum("hqk,khd->qhd", probs_low, heads_v, preferred_element_type=jnp.float32)
    attn_mix = attn_mix.reshape(full_len, block).astype(jnp.bfloat16)
    attn_part = jnp.dot(attn_mix, mat_out, preferred_element_type=jnp.float32)
    attn_out = lax.psum_scatter(
        attn_part.astype(jnp.bfloat16), "ctx", scatter_dimension=0, tiled=True
    )
    rows_loc = tokens_loc.astype(jnp.float32)
    resid_one = rows_loc + (attn_out.astype(jnp.float32) + bias_out)

    normed_two, ln_two_pull = jax.vjp(layer_norm, resid_one, gain_two, shift_two)
    hidden_two = lax.all_gather(normed_two.astype(jnp.bfloat16), "ctx", axis=0, tiled=True)
    up_pre = jnp.dot(hidden_two, mat_up, preferred_element_type=jnp.float32) + bias_up_own
    act_out, gelu_pull = jax.vjp(gelu_tanh, up_pre)
    act_low = act_out.astype(jnp.bfloat16)
    grad_act = times_trans(dy_all, mat_down)
    grad_up_low = gelu_pull(grad_act)[0].astype(jnp.bfloat16)
    grad_normed_part = times_trans(grad_up_low, mat_up).astype(jnp.bfloat16)
    grad_normed_two = lax.psum_scatter(grad_normed_part, "ctx", scatter_dimension=0, tiled=True)
    dy_loc = jnp.where(live_loc[:, None], grads_loc, jnp.zeros_like(grads_loc)).astype(jnp.float32)
    grad_bias_down = jnp.sum(dy_loc, axis=0)
    grad_bias_up = jnp.sum(grad_up_low.astype(jnp.float32), axis=0)
    grad_resid_ln, grad_gain_two, grad_shift_two = ln_two_pull(grad_normed_two.astype(jnp.float32))
    grad_resid = dy_loc + grad_resid_ln
    grad_attn_loc = grad_resid.astype(jnp.bfloat16)
    grad_bias_out = jnp.sum(grad_attn_loc.astype(jnp.float32), axis=0)
    grad_attn = lax.all_gather(grad_attn_loc, "ctx", axis=0, tiled=True)

    down_part = jnp.dot(act_low, mat_down, preferred_element_type=jnp.float32).astype(jnp.bfloat16)
    grad_attn, down_part = lax.optimization_barrier((grad_attn, down_part))
    down_out = lax.psum_scatter(down_part, "ctx", scatter_dimension=0, tiled=True)
    block_out = (resid_one + (down_out.astype(jnp.float32) + bias_down)).astype(jnp.bfloat16)[None]
    sum_up, sum_down = reduce_all(
        [
            outer_sum(hidden_two, grad_up_low)
            .astype(jnp.bfloat16)
            .reshape(parts, group, rows_in, hid),
            outer_sum(act_low, dy_all)
            .astype(jnp.bfloat16)
            .reshape(group, parts, -1, MODEL_WIDTH),
        ],
        (True, False),
        group,
        1,
    )

    grad_mixed = times_trans(grad_attn, mat_out).astype(jnp.bfloat16)
    grad_mixed = grad_mixed.reshape(full_len, heads, HEAD_DIM)
    grad_value = jnp.einsum(
        "hqk,qhd->khd", probs_low, grad_mixed, preferred_element_type=jnp.float32
    )
    grad_probs = jnp.einsum("qhd,khd->hqk", grad_mixed, heads_v, preferred_element_type=jnp.float32)
    grad_scores = probs_vals * (
        grad_probs - jnp.sum(probs_vals * grad_probs, axis=-1, keepdims=True)
    )
    grad_scores_low = grad_scores.astype(jnp.bfloat16)
    grad_query = (
        jnp.einsum("hqk,khd->qhd", grad_scores_low, heads_k, preferred_element_type=jnp.float32)
        * score_scale
    )
    grad_key = (
        jnp.einsum("hqk,qhd->khd", grad_scores_low, heads_q, preferred_element_type=jnp.float32)
        * score_scale
    )
    grad_qkv_low = jnp.concatenate(
        [part.reshape(full_len, block) for part in (grad_query, grad_key, grad_value)], axis=1
    ).astype(jnp.bfloat16)
    grad_bias_qkv = jnp.sum(grad_qkv_low.astype(jnp.float32), axis=0)
    grad_first_part = times_trans(grad_qkv_low, mat_qkv).astype(jnp.bfloat16)
    grad_normed_one = lax.psum_scatter(grad_first_part, "ctx", scatter_dimension=0, tiled=True)
    _, ln_one_pull = jax.vjp(layer_norm, rows_loc, gain_one, shift_one)
    grad_rows_ln, grad_gain_one, grad_shift_one = ln_one_pull(grad_normed_one.astype(jnp.float32))
    tokens_grad = (grad_resid + grad_rows_ln)[None]

    def own_columns(values, count):
        wide_all = jnp.zeros((count, parts, values.size // count), jnp.float32)
        return lax.dynamic_update_slice(
            wide_all, values.reshape(count, 1, -1), (0, own, 0)
        ).reshape(-1)

    grad_vec = jnp.concatenate(
        [
            grad_gain_one,
            grad_shift_one,
            own_columns(grad_bias_qkv, 3),
            grad_bias_out,
            grad_gain_two,
            grad_shift_two,
            own_columns(grad_bias_up, 1),
            grad_bias_down,
        ]
    )
    vec_pack = jnp.pad(
        grad_vec.reshape(parts, group, vec_len), ((0, 0), (0, 0), (0, 2048 - vec_len))
    ).reshape(parts, group, 16, 128)
    sum_qkv, sum_out, sum_vec = reduce_all(
        [
            outer_sum(hidden_one, grad_qkv_low)
            .astype(jnp.bfloat16)
            .reshape(parts, group, rows_in, wide_qkv),
            outer_sum(attn_mix, grad_attn)
            .astype(jnp.bfloat16)
            .reshape(group, 2, rows_out // 2, MODEL_WIDTH),
            vec_pack.astype(jnp.bfloat16),
        ],
        (True, False, True),
        group,
        2,
    )

    ffn_cols = lax.all_to_all(sum_up, "ctx", 0, 0)
    total_up = ffn_cols.transpose(1, 0, 2).reshape(w_up.shape).astype(jnp.float32)
    total_down = sum_down.reshape(w_down.shape).astype(jnp.float32)
    total_out = sum_out.reshape(w_attn_out.shape).astype(jnp.float32)
    qkv_cols = lax.all_to_all(
        jnp.concatenate(
            [sum_qkv, jnp.pad(sum_vec, ((0, 0), (0, 0), (0, wide_qkv - 128)))], axis=1
        ),
        "ctx",
        0,
        0,
    )
    total_qkv = (
        qkv_cols[:, :rows_in]
        .reshape(parts, rows_in, 3, block)
        .transpose(1, 2, 0, 3)
        .reshape(w_qkv.shape)
        .astype(jnp.float32)
    )
    total_vec = jnp.sum(qkv_cols[:, rows_in:, :128].astype(jnp.float32), axis=0).reshape(-1)[
        :vec_len
    ]
    new_qkv, mom_qkv, sec_qkv = adamw_update(
        w_qkv, total_qkv, momentum_qkv_weight, second_qkv, 0.05, 0.1
    )
    new_out, mom_out, sec_out = adamw_update(
        w_attn_out, total_out, momentum_attn_output, second_attn_out, 0.05, 0.1
    )
    new_up, mom_up, sec_up = adamw_update(w_up, total_up, momentum_up_weight, second_up, 0.05, 0.1)
    new_down, mom_down, sec_down = adamw_update(
        w_down, total_down, momentum_down_weight, second_down, 0.05, 0.1
    )
    new_vec, mom_vec, sec_vec = adamw_update(
        vectors, total_vec, momentum_vector_rows, second_vectors, 0.6, 0.0
    )
    return (
        block_out,
        tokens_grad,
        new_qkv,
        new_out,
        new_up,
        new_down,
        new_vec,
        mom_qkv,
        mom_out,
        mom_up,
        mom_down,
        mom_vec,
        sec_qkv,
        sec_out,
        sec_up,
        sec_down,
        sec_vec,
    )


def solution(mesh):
    placed = (
        P(("fsdp", "replica"), "ctx", None),
        P(("fsdp", "replica"), "ctx", None),
        P(("fsdp", "replica"), None),
        P(("fsdp", "replica")),
        P(("ctx", "fsdp"), None),
        P(("ctx", "fsdp"), None),
        P(("ctx", "fsdp"), None),
        P(("ctx", "fsdp"), None),
        P(("ctx", "fsdp")),
        P(("ctx", "fsdp"), None),
        P(("ctx", "fsdp"), None),
        P(("ctx", "fsdp"), None),
        P(("ctx", "fsdp"), None),
        P(("ctx", "fsdp")),
        P(("ctx", "fsdp"), None),
        P(("ctx", "fsdp"), None),
        P(("ctx", "fsdp"), None),
        P(("ctx", "fsdp"), None),
        P(("ctx", "fsdp")),
    )
    return jax.shard_map(
        shards,
        mesh=mesh,
        in_specs=placed,
        out_specs=(
            P(("fsdp", "replica"), "ctx", None),
            P(("fsdp", "replica"), "ctx", None),
            P(("ctx", "fsdp"), None),
            P(("ctx", "fsdp"), None),
            P(("ctx", "fsdp"), None),
            P(("ctx", "fsdp"), None),
            P(("ctx", "fsdp")),
            P(("ctx", "fsdp"), None),
            P(("ctx", "fsdp"), None),
            P(("ctx", "fsdp"), None),
            P(("ctx", "fsdp"), None),
            P(("ctx", "fsdp")),
            P(("ctx", "fsdp"), None),
            P(("ctx", "fsdp"), None),
            P(("ctx", "fsdp"), None),
            P(("ctx", "fsdp"), None),
            P(("ctx", "fsdp")),
        ),
        check_vma=False,
    )
```

```python
import functools

import jax
import jax.numpy as jnp
from jax import lax
from jax.experimental import pallas as pl
from jax.experimental.pallas import tpu as pltpu
from jax.sharding import PartitionSpec as P

MODEL_WIDTH = 1024
HEADS = 16
HEAD_DIM = 64
HIDDEN_UNITS = 4096
STEP = 10

MESH = pl.DeviceIdType.MESH


norm_eps = 1e-05
score_scale = 0.125
masked_score = -1e30
gelu_coef = 0.7978845608028654
beta_one = 0.9
beta_two = 0.95
adam_eps = 1e-08


def layer_norm(inputs, scale_vec, shift_vec):
    centre = inputs - jnp.mean(inputs, axis=-1, keepdims=True)
    spread = jnp.mean(centre * centre, axis=-1, keepdims=True)
    return centre * lax.rsqrt(spread + norm_eps) * scale_vec + shift_vec


def gelu_tanh(points):
    return (
        0.5 * points * (1.0 + jnp.tanh(gelu_coef * (points + 0.044715 * points * points * points)))
    )


def alibi_slopes(count_heads):
    return jnp.power(2.0, -8.0 * (jnp.arange(count_heads, dtype=jnp.float32) + 1.0) / count_heads)


def split_small(vector_all):
    bounds = [
        0,
        MODEL_WIDTH,
        2 * MODEL_WIDTH,
        5 * MODEL_WIDTH,
        6 * MODEL_WIDTH,
        7 * MODEL_WIDTH,
        8 * MODEL_WIDTH,
        8 * MODEL_WIDTH + HIDDEN_UNITS,
        9 * MODEL_WIDTH + HIDDEN_UNITS,
    ]
    return tuple(
        (vector_all[low_end:high_end] for low_end, high_end in zip(bounds[:-1], bounds[1:]))
    )


def outer_sum(left_mat, right_mat):
    return lax.dot_general(
        left_mat, right_mat, (((0,), (0,)), ((), ())), preferred_element_type=jnp.float32
    )


def times_trans(left_mat, right_mat):
    return lax.dot_general(
        left_mat, right_mat, (((1,), (1,)), ((), ())), preferred_element_type=jnp.float32
    )


def adamw_update(weight, gradient, first_mom, second, step_rate, decay_rate):
    first_new = beta_one * first_mom + (1.0 - beta_one) * gradient
    second_new = beta_two * second + (1.0 - beta_two) * gradient * gradient
    first_hat = first_new / (1.0 - beta_one**STEP)
    second_hat = second_new / (1.0 - beta_two**STEP)
    weight_new = weight - step_rate * (
        first_hat / (jnp.sqrt(second_hat) + adam_eps) + decay_rate * weight
    )
    return (weight_new, first_new, second_new)


def enter(group, me_f, me_r):
    barrier = pltpu.get_barrier_semaphore()
    for step in range(1, group):
        pl.semaphore_signal(
            barrier, inc=1, device_id={"fsdp": lax.rem(me_f + step, group)}, device_id_type=MESH
        )
    pl.semaphore_signal(barrier, inc=1, device_id={"replica": 1 - me_r}, device_id_type=MESH)
    pl.semaphore_wait(barrier, group)


def gather_kernel(group, kinds, *refs):
    count = len(kinds)
    ins, outs = refs[:count], refs[count : 2 * count]
    local_sem, send_sem, recv_sem, pass_send, pass_recv = refs[2 * count :]
    me_f, me_r = lax.axis_index("fsdp"), lax.axis_index("replica")
    enter(group, me_f, me_r)

    def spot(index, owner, half):
        if kinds[index]:
            return outs[index].at[half, owner]
        return outs[index].at[owner, half]

    halves, waits = [], []
    for index in range(count):
        size = ins[index].shape[0] // 2
        halves.append(pl.ds(me_r * size, size))
    for index in range(count):
        for step in range(1, group):
            copy = pltpu.make_async_remote_copy(
                src_ref=ins[index].at[halves[index]],
                dst_ref=spot(index, me_f, halves[index]),
                send_sem=send_sem.at[index, step - 1],
                recv_sem=recv_sem.at[index, step - 1],
                device_id={"fsdp": lax.rem(me_f + step, group)},
                device_id_type=MESH,
            )
            copy.start()
            waits.append((copy, index, step))
    own = []
    for index in range(count):
        whole = pl.ds(0, ins[index].shape[0])
        copy = pltpu.make_async_copy(ins[index], spot(index, me_f, whole), local_sem.at[index])
        copy.start()
        own.append(copy)
    passed = []
    for copy, index, step in waits:
        copy.wait_recv()
        sender = lax.rem(me_f + group - step, group)
        part = spot(index, sender, halves[index])
        onward = pltpu.make_async_remote_copy(
            src_ref=part,
            dst_ref=part,
            send_sem=pass_send.at[index, step - 1],
            recv_sem=pass_recv.at[index, step - 1],
            device_id={"replica": 1 - me_r},
            device_id_type=MESH,
        )
        onward.start()
        passed.append(onward)
    for copy, _, _ in waits:
        copy.wait_send()
    for copy in own:
        copy.wait()
    for copy in passed:
        copy.wait()


def gather_over_group(arrays, kinds, group):
    shapes = [
        (item.shape[0], group) + item.shape[1:] if kind else (group,) + item.shape
        for item, kind in zip(arrays, kinds)
    ]
    count = len(arrays)
    return pl.pallas_call(
        functools.partial(gather_kernel, group, kinds),
        out_shape=[
            jax.ShapeDtypeStruct(shape, item.dtype) for shape, item in zip(shapes, arrays)
        ],
        in_specs=[pl.BlockSpec(memory_space=pl.ANY)] * count,
        out_specs=[pl.BlockSpec(memory_space=pl.ANY)] * count,
        scratch_shapes=[pltpu.SemaphoreType.DMA((count,))]
        + [pltpu.SemaphoreType.DMA((count, group - 1))] * 4,
        compiler_params=pltpu.CompilerParams(collective_id=0, has_side_effects=True),
        cost_estimate=pl.CostEstimate(flops=0, bytes_accessed=120_000_000, transcendentals=0),
    )(*arrays)


def reduce_kernel(group, kinds, *refs):
    count = len(kinds)
    ins, outs = refs[:count], refs[count : 2 * count]
    firsts, seconds = refs[2 * count : 3 * count], refs[3 * count : 4 * count]
    core_send, core_recv, send_sem, recv_sem, pass_send, pass_recv = refs[4 * count :]
    me_f, me_r = lax.axis_index("fsdp"), lax.axis_index("replica")
    enter(group, me_f, me_r)
    sizes = [out.shape[0] // 2 for out in outs]

    def core_copy(source, target, sends, recvs, index):
        return pltpu.make_async_remote_copy(
            src_ref=source,
            dst_ref=target,
            send_sem=sends.at[index],
            recv_sem=recvs.at[index],
            device_id={"replica": 1 - me_r},
            device_id_type=MESH,
        )

    def at(ref, index, half, owner):
        return ref.at[half, owner] if kinds[index] else ref.at[owner, half]

    every = pl.ds(0, group)
    first_copies = []
    for index in range(count):
        other = pl.ds((1 - me_r) * sizes[index], sizes[index])
        copy = core_copy(
            at(ins[index], index, other, every), firsts[index], core_send, core_recv, index
        )
        copy.start()
        first_copies.append(copy)
    peer_copies = []
    for index in range(count):
        first_copies[index].wait_recv()
        for step in list(range(1, group)) + [0]:
            owner = lax.rem(me_f + step, group)

            def add(place, carry, index=index, owner=owner):
                here = at(firsts[index], index, place, owner)
                mine = at(ins[index], index, me_r * sizes[index] + place, owner)
                here[...] = (
                    here[...].astype(jnp.float32) + mine[...].astype(jnp.float32)
                ).astype(here.dtype)
                return carry

            lax.fori_loop(0, sizes[index], add, 0)
            if step:
                copy = pltpu.make_async_remote_copy(
                    src_ref=at(firsts[index], index, pl.ds(0, sizes[index]), owner),
                    dst_ref=seconds[index].at[step - 1],
                    send_sem=send_sem.at[index, step - 1],
                    recv_sem=recv_sem.at[index, step - 1],
                    device_id={"fsdp": owner},
                    device_id_type=MESH,
                )
                copy.start()
                peer_copies.append(copy)
    last_copies = []
    for index in range(count):
        for step in range(1, group):
            peer_copies[index * (group - 1) + step - 1].wait_recv()

        def total(place, carry, index=index):
            value = at(firsts[index], index, place, me_f)[...].astype(jnp.float32)
            for step in range(1, group):
                value += seconds[index][step - 1, place].astype(jnp.float32)
            outs[index][me_r * sizes[index] + place] = value.astype(outs[index].dtype)
            return carry

        lax.fori_loop(0, sizes[index], total, 0)
        part = outs[index].at[pl.ds(me_r * sizes[index], sizes[index])]
        copy = core_copy(part, part, pass_send, pass_recv, index)
        copy.start()
        last_copies.append(copy)
    for copy in first_copies + peer_copies:
        copy.wait_send()
    for copy in last_copies:
        copy.wait()


def reduce_over_group(arrays, kinds, group, name):
    count = len(arrays)
    outs, firsts, seconds = [], [], []
    for item, kind in zip(arrays, kinds):
        lead = item.shape[0] if kind else item.shape[1]
        rest = item.shape[2:]
        outs.append((lead,) + rest)
        half = lead // 2
        firsts.append(((half, group) if kind else (group, half)) + rest)
        seconds.append((group - 1, half) + rest)
    return pl.pallas_call(
        functools.partial(reduce_kernel, group, kinds),
        out_shape=[
            jax.ShapeDtypeStruct(shape, item.dtype) for shape, item in zip(outs, arrays)
        ],
        in_specs=[pl.BlockSpec(memory_space=pltpu.VMEM)] * count,
        out_specs=[pl.BlockSpec(memory_space=pltpu.VMEM)] * count,
        scratch_shapes=[
            pltpu.VMEM(shape, item.dtype) for shape, item in zip(firsts + seconds, arrays + arrays)
        ]
        + [pltpu.SemaphoreType.DMA((count,))] * 2
        + [pltpu.SemaphoreType.DMA((count, group - 1))] * 2
        + [pltpu.SemaphoreType.DMA((count,))] * 2,
        compiler_params=pltpu.CompilerParams(
            collective_id=name, has_side_effects=True, vmem_limit_bytes=24 * 1024 * 1024
        ),
        cost_estimate=pl.CostEstimate(
            flops=0,
            bytes_accessed=20_000_000 + 20 * sum(item.size for item in arrays),
            transcendentals=0,
        ),
    )(*arrays)


def plain_gather(arrays, kinds, group):
    return [
        lax.all_gather(item, "fsdp", axis=1 if kind else 0, tiled=False)
        for item, kind in zip(arrays, kinds)
    ]


def plain_reduce(arrays, kinds, group, name):
    return [
        lax.psum(lax.psum_scatter(item, "fsdp", scatter_dimension=1 if kind else 0), "replica")
        for item, kind in zip(arrays, kinds)
    ]


def shards(
    tokens,
    output_gradient,
    segment_ids,
    row_fill,
    w_qkv,
    w_attn_out,
    w_up,
    w_down,
    vectors,
    momentum_qkv_weight,
    momentum_attn_output,
    momentum_up_weight,
    momentum_down_weight,
    momentum_vector_rows,
    second_qkv,
    second_attn_out,
    second_up,
    second_down,
    second_vectors,
):
    parts, group = lax.axis_size("ctx"), lax.axis_size("fsdp")
    own = lax.axis_index("ctx")
    block = MODEL_WIDTH // parts
    hid = HIDDEN_UNITS // parts
    heads = HEADS // parts
    rows_in, rows_out, vec_len = w_qkv.shape[0], w_attn_out.shape[0], vectors.shape[0]
    paired = lax.axis_size("replica") == 2
    gather_all = gather_over_group if paired else plain_gather
    reduce_all = reduce_over_group if paired else plain_reduce
    wide_qkv = 3 * block
    tokens_loc, grads_loc = tokens[0], output_gradient[0]
    length = tokens_loc.shape[0]
    seg_row = segment_ids[0]
    full_len = seg_row.shape[0]
    place_all = jnp.arange(full_len, dtype=jnp.int32)
    live_all = place_all < row_fill[0]
    place_loc = own * length + jnp.arange(length, dtype=jnp.int32)
    live_loc = place_loc < row_fill[0]

    rows_all = lax.all_gather(tokens_loc, "ctx", axis=0, tiled=True)
    dy_all = lax.all_gather(grads_loc, "ctx", axis=0, tiled=True)

    vec_tile = jnp.pad(vectors.astype(jnp.bfloat16), (0, 2048 - vec_len)).reshape(16, 128)
    vec_tile = jnp.pad(vec_tile, ((0, 0), (0, wide_qkv + hid - 128)))
    send = jnp.concatenate(
        [
            w_qkv.astype(jnp.bfloat16)
            .reshape(rows_in, 3, parts, block)
            .transpose(2, 0, 1, 3)
            .reshape(parts, rows_in, wide_qkv),
            w_up.astype(jnp.bfloat16).reshape(rows_in, parts, hid).transpose(1, 0, 2),
        ],
        axis=2,
    )
    send = jnp.concatenate(
        [send, jnp.broadcast_to(vec_tile[None], (parts,) + vec_tile.shape)], axis=1
    )
    cols = lax.all_to_all(send, "ctx", 0, 0)
    mat_qkv, mat_out, mat_up, mat_down, vec_full = gather_all(
        [
            cols[:, :rows_in, :wide_qkv],
            w_attn_out.astype(jnp.bfloat16).reshape(2, rows_out // 2, MODEL_WIDTH),
            cols[:, :rows_in, wide_qkv:],
            w_down.astype(jnp.bfloat16).reshape(parts, -1, MODEL_WIDTH),
            cols[:, rows_in:, :128],
        ],
        (True, False, True, False, True),
        group,
    )
    rows_all, dy_all, mat_qkv, vec_full = lax.optimization_barrier(
        (rows_all, dy_all, mat_qkv, vec_full)
    )
    rows_all = rows_all.astype(jnp.float32)
    dy_all = jnp.where(live_all[:, None], dy_all, jnp.zeros_like(dy_all))
    mat_qkv = mat_qkv.reshape(MODEL_WIDTH, wide_qkv)
    mat_up = mat_up.reshape(MODEL_WIDTH, hid)
    mat_down = mat_down.reshape(hid, MODEL_WIDTH)
    mat_out = mat_out.reshape(block, MODEL_WIDTH)
    vec_full = vec_full.reshape(parts * group, 2048)[:, :vec_len].reshape(-1)
    gain_one, shift_one, bias_qkv, bias_out, gain_two, shift_two, bias_up, bias_down = split_small(
        vec_full.astype(jnp.float32)
    )
    bias_qkv_own = lax.dynamic_slice_in_dim(
        bias_qkv.reshape(3, MODEL_WIDTH), own * block, block, axis=1
    ).reshape(-1)
    bias_up_own = lax.dynamic_slice_in_dim(bias_up, own * hid, hid)

    normed_one = layer_norm(rows_all, gain_one, shift_one)
    hidden_one = normed_one.astype(jnp.bfloat16)
    qkv_low = (
        jnp.dot(hidden_one, mat_qkv, preferred_element_type=jnp.float32) + bias_qkv_own
    ).astype(jnp.bfloat16)
    heads_q = qkv_low[:, :block].reshape(full_len, heads, HEAD_DIM)
    heads_k = qkv_low[:, block : 2 * block].reshape(full_len, heads, HEAD_DIM)
    heads_v = qkv_low[:, 2 * block :].reshape(full_len, heads, HEAD_DIM)
    allowed = (place_all[None, :] <= place_all[:, None]) & (seg_row[:, None] == seg_row[None, :])
    distance = (place_all[:, None] - place_all[None, :]).astype(jnp.float32)
    slopes = lax.dynamic_slice_in_dim(alibi_slopes(HEADS), own * heads, heads)
    scores = (
        jnp.einsum("qhd,khd->hqk", heads_q, heads_k, preferred_element_type=jnp.float32)
        * score_scale
        - slopes[:, None, None] * distance[None]
    )
    scores = jnp.where(allowed[None], scores, masked_score)
    row_max = jnp.max(scores, axis=-1, keepdims=True)
    exp_scores = jnp.exp(scores - row_max)
    probs_vals = exp_scores / jnp.sum(exp_scores, axis=-1, keepdims=True)
    probs_low = probs_vals.astype(jnp.bfloat16)
    attn_mix = jnp.einsum("hqk,khd->qhd", probs_low, heads_v, preferred_element_type=jnp.float32)
    attn_mix = attn_mix.reshape(full_len, block).astype(jnp.bfloat16)
    attn_part = jnp.dot(attn_mix, mat_out, preferred_element_type=jnp.float32)
    attn_out = lax.psum_scatter(
        attn_part.astype(jnp.bfloat16), "ctx", scatter_dimension=0, tiled=True
    )
    rows_loc = tokens_loc.astype(jnp.float32)
    resid_one = rows_loc + (attn_out.astype(jnp.float32) + bias_out)

    normed_two, ln_two_pull = jax.vjp(layer_norm, resid_one, gain_two, shift_two)
    hidden_two = lax.all_gather(normed_two.astype(jnp.bfloat16), "ctx", axis=0, tiled=True)
    up_pre = jnp.dot(hidden_two, mat_up, preferred_element_type=jnp.float32) + bias_up_own
    act_out, gelu_pull = jax.vjp(gelu_tanh, up_pre)
    act_low = act_out.astype(jnp.bfloat16)
    grad_act = times_trans(dy_all, mat_down)
    grad_up_low = gelu_pull(grad_act)[0].astype(jnp.bfloat16)
    grad_normed_part = times_trans(grad_up_low, mat_up).astype(jnp.bfloat16)
    grad_normed_two = lax.psum_scatter(grad_normed_part, "ctx", scatter_dimension=0, tiled=True)
    dy_loc = jnp.where(live_loc[:, None], grads_loc, jnp.zeros_like(grads_loc)).astype(jnp.float32)
    grad_bias_down = jnp.sum(dy_loc, axis=0)
    grad_bias_up = jnp.sum(grad_up_low.astype(jnp.float32), axis=0)
    grad_resid_ln, grad_gain_two, grad_shift_two = ln_two_pull(grad_normed_two.astype(jnp.float32))
    grad_resid = dy_loc + grad_resid_ln
    grad_attn_loc = grad_resid.astype(jnp.bfloat16)
    grad_bias_out = jnp.sum(grad_attn_loc.astype(jnp.float32), axis=0)
    grad_attn = lax.all_gather(grad_attn_loc, "ctx", axis=0, tiled=True)

    down_part = jnp.dot(act_low, mat_down, preferred_element_type=jnp.float32).astype(jnp.bfloat16)
    grad_attn, down_part = lax.optimization_barrier((grad_attn, down_part))
    down_out = lax.psum_scatter(down_part, "ctx", scatter_dimension=0, tiled=True)
    block_out = (resid_one + (down_out.astype(jnp.float32) + bias_down)).astype(jnp.bfloat16)[None]
    sum_up, sum_down = reduce_all(
        [
            outer_sum(hidden_two, grad_up_low)
            .astype(jnp.bfloat16)
            .reshape(parts, group, rows_in, hid),
            outer_sum(act_low, dy_all)
            .astype(jnp.bfloat16)
            .reshape(group, parts, -1, MODEL_WIDTH),
        ],
        (True, False),
        group,
        1,
    )

    grad_mixed = times_trans(grad_attn, mat_out).astype(jnp.bfloat16)
    grad_mixed = grad_mixed.reshape(full_len, heads, HEAD_DIM)
    grad_value = jnp.einsum(
        "hqk,qhd->khd", probs_low, grad_mixed, preferred_element_type=jnp.float32
    )
    grad_probs = jnp.einsum("qhd,khd->hqk", grad_mixed, heads_v, preferred_element_type=jnp.float32)
    grad_scores = probs_vals * (
        grad_probs - jnp.sum(probs_vals * grad_probs, axis=-1, keepdims=True)
    )
    grad_scores_low = grad_scores.astype(jnp.bfloat16)
    grad_query = (
        jnp.einsum("hqk,khd->qhd", grad_scores_low, heads_k, preferred_element_type=jnp.float32)
        * score_scale
    )
    grad_key = (
        jnp.einsum("hqk,qhd->khd", grad_scores_low, heads_q, preferred_element_type=jnp.float32)
        * score_scale
    )
    grad_qkv_low = jnp.concatenate(
        [part.reshape(full_len, block) for part in (grad_query, grad_key, grad_value)], axis=1
    ).astype(jnp.bfloat16)
    grad_bias_qkv = jnp.sum(grad_qkv_low.astype(jnp.float32), axis=0)
    grad_first_part = times_trans(grad_qkv_low, mat_qkv).astype(jnp.bfloat16)
    grad_normed_one = lax.psum_scatter(grad_first_part, "ctx", scatter_dimension=0, tiled=True)
    _, ln_one_pull = jax.vjp(layer_norm, rows_loc, gain_one, shift_one)
    grad_rows_ln, grad_gain_one, grad_shift_one = ln_one_pull(grad_normed_one.astype(jnp.float32))
    tokens_grad = (grad_resid + grad_rows_ln)[None]

    def own_columns(values, count):
        wide_all = jnp.zeros((count, parts, values.size // count), jnp.float32)
        return lax.dynamic_update_slice(
            wide_all, values.reshape(count, 1, -1), (0, own, 0)
        ).reshape(-1)

    grad_vec = jnp.concatenate(
        [
            grad_gain_one,
            grad_shift_one,
            own_columns(grad_bias_qkv, 3),
            grad_bias_out,
            grad_gain_two,
            grad_shift_two,
            own_columns(grad_bias_up, 1),
            grad_bias_down,
        ]
    )
    vec_pack = jnp.pad(
        grad_vec.reshape(parts, group, vec_len), ((0, 0), (0, 0), (0, 2048 - vec_len))
    ).reshape(parts, group, 16, 128)
    sum_qkv, sum_out = reduce_all(
        [
            outer_sum(hidden_one, grad_qkv_low)
            .astype(jnp.bfloat16)
            .reshape(parts, group, rows_in, wide_qkv),
            outer_sum(attn_mix, grad_attn)
            .astype(jnp.bfloat16)
            .reshape(group, 2, rows_out // 2, MODEL_WIDTH),
        ],
        (True, False),
        group,
        2,
    )
    (sum_vec,) = reduce_all([vec_pack.astype(jnp.bfloat16)], (True,), group, 3)

    ffn_cols = lax.all_to_all(sum_up, "ctx", 0, 0)
    total_up = ffn_cols.transpose(1, 0, 2).reshape(w_up.shape).astype(jnp.float32)
    total_down = sum_down.reshape(w_down.shape).astype(jnp.float32)
    total_out = sum_out.reshape(w_attn_out.shape).astype(jnp.float32)
    qkv_cols = lax.all_to_all(sum_qkv, "ctx", 0, 0)
    vec_cols = lax.all_to_all(sum_vec, "ctx", 0, 0)
    total_qkv = (
        qkv_cols.reshape(parts, rows_in, 3, block)
        .transpose(1, 2, 0, 3)
        .reshape(w_qkv.shape)
        .astype(jnp.float32)
    )
    total_vec = jnp.sum(vec_cols.astype(jnp.float32), axis=0).reshape(-1)[:vec_len]
    new_qkv, mom_qkv, sec_qkv = adamw_update(
        w_qkv, total_qkv, momentum_qkv_weight, second_qkv, 0.05, 0.1
    )
    new_out, mom_out, sec_out = adamw_update(
        w_attn_out, total_out, momentum_attn_output, second_attn_out, 0.05, 0.1
    )
    new_up, mom_up, sec_up = adamw_update(w_up, total_up, momentum_up_weight, second_up, 0.05, 0.1)
    new_down, mom_down, sec_down = adamw_update(
        w_down, total_down, momentum_down_weight, second_down, 0.05, 0.1
    )
    new_vec, mom_vec, sec_vec = adamw_update(
        vectors, total_vec, momentum_vector_rows, second_vectors, 0.6, 0.0
    )
    return (
        block_out,
        tokens_grad,
        new_qkv,
        new_out,
        new_up,
        new_down,
        new_vec,
        mom_qkv,
        mom_out,
        mom_up,
        mom_down,
        mom_vec,
        sec_qkv,
        sec_out,
        sec_up,
        sec_down,
        sec_vec,
    )


def solution(mesh):
    placed = (
        P(("fsdp", "replica"), "ctx", None),
        P(("fsdp", "replica"), "ctx", None),
        P(("fsdp", "replica"), None),
        P(("fsdp", "replica")),
        P(("ctx", "fsdp"), None),
        P(("ctx", "fsdp"), None),
        P(("ctx", "fsdp"), None),
        P(("ctx", "fsdp"), None),
        P(("ctx", "fsdp")),
        P(("ctx", "fsdp"), None),
        P(("ctx", "fsdp"), None),
        P(("ctx", "fsdp"), None),
        P(("ctx", "fsdp"), None),
        P(("ctx", "fsdp")),
        P(("ctx", "fsdp"), None),
        P(("ctx", "fsdp"), None),
        P(("ctx", "fsdp"), None),
        P(("ctx", "fsdp"), None),
        P(("ctx", "fsdp")),
    )
    return jax.shard_map(
        shards,
        mesh=mesh,
        in_specs=placed,
        out_specs=(
            P(("fsdp", "replica"), "ctx", None),
            P(("fsdp", "replica"), "ctx", None),
            P(("ctx", "fsdp"), None),
            P(("ctx", "fsdp"), None),
            P(("ctx", "fsdp"), None),
            P(("ctx", "fsdp"), None),
            P(("ctx", "fsdp")),
            P(("ctx", "fsdp"), None),
            P(("ctx", "fsdp"), None),
            P(("ctx", "fsdp"), None),
            P(("ctx", "fsdp"), None),
            P(("ctx", "fsdp")),
            P(("ctx", "fsdp"), None),
            P(("ctx", "fsdp"), None),
            P(("ctx", "fsdp"), None),
            P(("ctx", "fsdp"), None),
            P(("ctx", "fsdp")),
        ),
        check_vma=False,
    )
```

```python
import functools

import jax
import jax.numpy as jnp
from jax import lax
from jax.experimental import pallas as pl
from jax.experimental.pallas import tpu as pltpu
from jax.sharding import PartitionSpec as P

MODEL_WIDTH = 1024
HEADS = 16
HEAD_DIM = 64
HIDDEN_UNITS = 4096
STEP = 10

MESH = pl.DeviceIdType.MESH


norm_eps = 1e-05
score_scale = 0.125
masked_score = -1e30
gelu_coef = 0.7978845608028654
beta_one = 0.9
beta_two = 0.95
adam_eps = 1e-08


def layer_norm(inputs, scale_vec, shift_vec):
    centre = inputs - jnp.mean(inputs, axis=-1, keepdims=True)
    spread = jnp.mean(centre * centre, axis=-1, keepdims=True)
    return centre * lax.rsqrt(spread + norm_eps) * scale_vec + shift_vec


def gelu_tanh(points):
    return (
        0.5 * points * (1.0 + jnp.tanh(gelu_coef * (points + 0.044715 * points * points * points)))
    )


def alibi_slopes(count_heads):
    return jnp.power(2.0, -8.0 * (jnp.arange(count_heads, dtype=jnp.float32) + 1.0) / count_heads)


def split_small(vector_all):
    bounds = [
        0,
        MODEL_WIDTH,
        2 * MODEL_WIDTH,
        5 * MODEL_WIDTH,
        6 * MODEL_WIDTH,
        7 * MODEL_WIDTH,
        8 * MODEL_WIDTH,
        8 * MODEL_WIDTH + HIDDEN_UNITS,
        9 * MODEL_WIDTH + HIDDEN_UNITS,
    ]
    return tuple(
        (vector_all[low_end:high_end] for low_end, high_end in zip(bounds[:-1], bounds[1:]))
    )


def outer_sum(left_mat, right_mat):
    return lax.dot_general(
        left_mat, right_mat, (((0,), (0,)), ((), ())), preferred_element_type=jnp.float32
    )


def times_trans(left_mat, right_mat):
    return lax.dot_general(
        left_mat, right_mat, (((1,), (1,)), ((), ())), preferred_element_type=jnp.float32
    )


def adamw_update(weight, gradient, first_mom, second, step_rate, decay_rate):
    first_new = beta_one * first_mom + (1.0 - beta_one) * gradient
    second_new = beta_two * second + (1.0 - beta_two) * gradient * gradient
    first_hat = first_new / (1.0 - beta_one**STEP)
    second_hat = second_new / (1.0 - beta_two**STEP)
    weight_new = weight - step_rate * (
        first_hat / (jnp.sqrt(second_hat) + adam_eps) + decay_rate * weight
    )
    return (weight_new, first_new, second_new)


def enter(group, me_f, me_r):
    barrier = pltpu.get_barrier_semaphore()
    for step in range(1, group):
        pl.semaphore_signal(
            barrier, inc=1, device_id={"fsdp": lax.rem(me_f + step, group)}, device_id_type=MESH
        )
    pl.semaphore_signal(barrier, inc=1, device_id={"replica": 1 - me_r}, device_id_type=MESH)
    pl.semaphore_wait(barrier, group)


def gather_kernel(group, kinds, *refs):
    count = len(kinds)
    ins, outs = refs[:count], refs[count : 2 * count]
    local_sem, send_sem, recv_sem, pass_send, pass_recv = refs[2 * count :]
    me_f, me_r = lax.axis_index("fsdp"), lax.axis_index("replica")
    enter(group, me_f, me_r)

    def spot(index, owner, half):
        if kinds[index]:
            return outs[index].at[half, owner]
        return outs[index].at[owner, half]

    halves, waits = [], []
    for index in range(count):
        size = ins[index].shape[0] // 2
        halves.append(pl.ds(me_r * size, size))
    for index in range(count):
        for step in range(1, group):
            copy = pltpu.make_async_remote_copy(
                src_ref=ins[index].at[halves[index]],
                dst_ref=spot(index, me_f, halves[index]),
                send_sem=send_sem.at[index, step - 1],
                recv_sem=recv_sem.at[index, step - 1],
                device_id={"fsdp": lax.rem(me_f + step, group)},
                device_id_type=MESH,
            )
            copy.start()
            waits.append((copy, index, step))
    own = []
    for index in range(count):
        whole = pl.ds(0, ins[index].shape[0])
        copy = pltpu.make_async_copy(ins[index], spot(index, me_f, whole), local_sem.at[index])
        copy.start()
        own.append(copy)
    passed = []
    for copy, index, step in waits:
        copy.wait_recv()
        sender = lax.rem(me_f + group - step, group)
        part = spot(index, sender, halves[index])
        onward = pltpu.make_async_remote_copy(
            src_ref=part,
            dst_ref=part,
            send_sem=pass_send.at[index, step - 1],
            recv_sem=pass_recv.at[index, step - 1],
            device_id={"replica": 1 - me_r},
            device_id_type=MESH,
        )
        onward.start()
        passed.append(onward)
    for copy, _, _ in waits:
        copy.wait_send()
    for copy in own:
        copy.wait()
    for copy in passed:
        copy.wait()


def gather_over_group(arrays, kinds, group):
    shapes = [
        (item.shape[0], group) + item.shape[1:] if kind else (group,) + item.shape
        for item, kind in zip(arrays, kinds)
    ]
    count = len(arrays)
    return pl.pallas_call(
        functools.partial(gather_kernel, group, kinds),
        out_shape=[
            jax.ShapeDtypeStruct(shape, item.dtype) for shape, item in zip(shapes, arrays)
        ],
        in_specs=[pl.BlockSpec(memory_space=pl.ANY)] * count,
        out_specs=[pl.BlockSpec(memory_space=pl.ANY)] * count,
        scratch_shapes=[pltpu.SemaphoreType.DMA((count,))]
        + [pltpu.SemaphoreType.DMA((count, group - 1))] * 4,
        compiler_params=pltpu.CompilerParams(collective_id=0, has_side_effects=True),
        cost_estimate=pl.CostEstimate(flops=0, bytes_accessed=120_000_000, transcendentals=0),
    )(*arrays)


def reduce_kernel(group, kinds, *refs):
    count = len(kinds)
    ins, outs = refs[:count], refs[count : 2 * count]
    firsts, seconds = refs[2 * count : 3 * count], refs[3 * count : 4 * count]
    core_send, core_recv, send_sem, recv_sem, pass_send, pass_recv = refs[4 * count :]
    me_f, me_r = lax.axis_index("fsdp"), lax.axis_index("replica")
    enter(group, me_f, me_r)
    sizes = [out.shape[0] // 2 for out in outs]

    def core_copy(source, target, sends, recvs, index):
        return pltpu.make_async_remote_copy(
            src_ref=source,
            dst_ref=target,
            send_sem=sends.at[index],
            recv_sem=recvs.at[index],
            device_id={"replica": 1 - me_r},
            device_id_type=MESH,
        )

    def at(ref, index, half, owner):
        return ref.at[half, owner] if kinds[index] else ref.at[owner, half]

    every = pl.ds(0, group)
    first_copies = []
    for index in range(count):
        other = pl.ds((1 - me_r) * sizes[index], sizes[index])
        copy = core_copy(
            at(ins[index], index, other, every), firsts[index], core_send, core_recv, index
        )
        copy.start()
        first_copies.append(copy)
    peer_copies = []
    for index in range(count):
        first_copies[index].wait_recv()
        for step in list(range(1, group)) + [0]:
            owner = lax.rem(me_f + step, group)

            def add(place, carry, index=index, owner=owner):
                here = at(firsts[index], index, place, owner)
                mine = at(ins[index], index, me_r * sizes[index] + place, owner)
                here[...] = (
                    here[...].astype(jnp.float32) + mine[...].astype(jnp.float32)
                ).astype(here.dtype)
                return carry

            lax.fori_loop(0, sizes[index], add, 0)
            if step:
                copy = pltpu.make_async_remote_copy(
                    src_ref=at(firsts[index], index, pl.ds(0, sizes[index]), owner),
                    dst_ref=seconds[index].at[step - 1],
                    send_sem=send_sem.at[index, step - 1],
                    recv_sem=recv_sem.at[index, step - 1],
                    device_id={"fsdp": owner},
                    device_id_type=MESH,
                )
                copy.start()
                peer_copies.append(copy)
    last_copies = []
    for index in range(count):
        for step in range(1, group):
            peer_copies[index * (group - 1) + step - 1].wait_recv()

        def total(place, carry, index=index):
            value = at(firsts[index], index, place, me_f)[...].astype(jnp.float32)
            for step in range(1, group):
                value += seconds[index][step - 1, place].astype(jnp.float32)
            outs[index][me_r * sizes[index] + place] = value.astype(outs[index].dtype)
            return carry

        lax.fori_loop(0, sizes[index], total, 0)
        part = outs[index].at[pl.ds(me_r * sizes[index], sizes[index])]
        copy = core_copy(part, part, pass_send, pass_recv, index)
        copy.start()
        last_copies.append(copy)
    for copy in first_copies + peer_copies:
        copy.wait_send()
    for copy in last_copies:
        copy.wait()


def reduce_over_group(arrays, kinds, group, name):
    count = len(arrays)
    outs, firsts, seconds = [], [], []
    for item, kind in zip(arrays, kinds):
        lead = item.shape[0] if kind else item.shape[1]
        rest = item.shape[2:]
        outs.append((lead,) + rest)
        half = lead // 2
        firsts.append(((half, group) if kind else (group, half)) + rest)
        seconds.append((group - 1, half) + rest)
    return pl.pallas_call(
        functools.partial(reduce_kernel, group, kinds),
        out_shape=[
            jax.ShapeDtypeStruct(shape, item.dtype) for shape, item in zip(outs, arrays)
        ],
        in_specs=[pl.BlockSpec(memory_space=pltpu.VMEM)] * count,
        out_specs=[pl.BlockSpec(memory_space=pltpu.VMEM)] * count,
        scratch_shapes=[
            pltpu.VMEM(shape, item.dtype) for shape, item in zip(firsts + seconds, arrays + arrays)
        ]
        + [pltpu.SemaphoreType.DMA((count,))] * 2
        + [pltpu.SemaphoreType.DMA((count, group - 1))] * 2
        + [pltpu.SemaphoreType.DMA((count,))] * 2,
        compiler_params=pltpu.CompilerParams(
            collective_id=name, has_side_effects=True, vmem_limit_bytes=24 * 1024 * 1024
        ),
        cost_estimate=pl.CostEstimate(
            flops=0,
            bytes_accessed=20_000_000 + 20 * sum(item.size for item in arrays),
            transcendentals=0,
        ),
    )(*arrays)


def plain_gather(arrays, kinds, group):
    return [
        lax.all_gather(item, "fsdp", axis=1 if kind else 0, tiled=False)
        for item, kind in zip(arrays, kinds)
    ]


def plain_reduce(arrays, kinds, group, name):
    return [
        lax.psum(lax.psum_scatter(item, "fsdp", scatter_dimension=1 if kind else 0), "replica")
        for item, kind in zip(arrays, kinds)
    ]


def shards(
    tokens,
    output_gradient,
    segment_ids,
    row_fill,
    w_qkv,
    w_attn_out,
    w_up,
    w_down,
    vectors,
    momentum_qkv_weight,
    momentum_attn_output,
    momentum_up_weight,
    momentum_down_weight,
    momentum_vector_rows,
    second_qkv,
    second_attn_out,
    second_up,
    second_down,
    second_vectors,
):
    parts, group = lax.axis_size("ctx"), lax.axis_size("fsdp")
    own = lax.axis_index("ctx")
    block = MODEL_WIDTH // parts
    hid = HIDDEN_UNITS // parts
    heads = HEADS // parts
    rows_in, rows_out, vec_len = w_qkv.shape[0], w_attn_out.shape[0], vectors.shape[0]
    paired = lax.axis_size("replica") == 2
    gather_all = gather_over_group if paired else plain_gather
    reduce_all = reduce_over_group if paired else plain_reduce
    wide_qkv = 3 * block
    tokens_loc, grads_loc = tokens[0], output_gradient[0]
    length = tokens_loc.shape[0]
    seg_row = segment_ids[0]
    full_len = seg_row.shape[0]
    place_all = jnp.arange(full_len, dtype=jnp.int32)
    live_all = place_all < row_fill[0]
    place_loc = own * length + jnp.arange(length, dtype=jnp.int32)
    live_loc = place_loc < row_fill[0]


    vec_tile = jnp.pad(vectors.astype(jnp.bfloat16), (0, 2048 - vec_len)).reshape(16, 128)
    vec_tile = jnp.pad(vec_tile, ((0, 0), (0, wide_qkv + hid - 128)))
    send = jnp.concatenate(
        [
            w_qkv.astype(jnp.bfloat16)
            .reshape(rows_in, 3, parts, block)
            .transpose(2, 0, 1, 3)
            .reshape(parts, rows_in, wide_qkv),
            w_up.astype(jnp.bfloat16).reshape(rows_in, parts, hid).transpose(1, 0, 2),
        ],
        axis=2,
    )
    send = jnp.concatenate(
        [send, jnp.broadcast_to(vec_tile[None], (parts,) + vec_tile.shape)], axis=1
    )
    cols = lax.all_to_all(send, "ctx", 0, 0)
    cols, tokens_next, grads_next = lax.optimization_barrier((cols, tokens_loc, grads_loc))
    rows_all = lax.all_gather(tokens_next, "ctx", axis=0, tiled=True)
    dy_all = lax.all_gather(grads_next, "ctx", axis=0, tiled=True)
    mat_qkv, mat_out, mat_up, mat_down, vec_full = gather_all(
        [
            cols[:, :rows_in, :wide_qkv],
            w_attn_out.astype(jnp.bfloat16).reshape(2, rows_out // 2, MODEL_WIDTH),
            cols[:, :rows_in, wide_qkv:],
            w_down.astype(jnp.bfloat16).reshape(parts, -1, MODEL_WIDTH),
            cols[:, rows_in:, :128],
        ],
        (True, False, True, False, True),
        group,
    )
    rows_all, dy_all, mat_qkv, vec_full = lax.optimization_barrier(
        (rows_all, dy_all, mat_qkv, vec_full)
    )
    rows_all = rows_all.astype(jnp.float32)
    dy_all = jnp.where(live_all[:, None], dy_all, jnp.zeros_like(dy_all))
    mat_qkv = mat_qkv.reshape(MODEL_WIDTH, wide_qkv)
    mat_up = mat_up.reshape(MODEL_WIDTH, hid)
    mat_down = mat_down.reshape(hid, MODEL_WIDTH)
    mat_out = mat_out.reshape(block, MODEL_WIDTH)
    vec_full = vec_full.reshape(parts * group, 2048)[:, :vec_len].reshape(-1)
    gain_one, shift_one, bias_qkv, bias_out, gain_two, shift_two, bias_up, bias_down = split_small(
        vec_full.astype(jnp.float32)
    )
    bias_qkv_own = lax.dynamic_slice_in_dim(
        bias_qkv.reshape(3, MODEL_WIDTH), own * block, block, axis=1
    ).reshape(-1)
    bias_up_own = lax.dynamic_slice_in_dim(bias_up, own * hid, hid)

    normed_one = layer_norm(rows_all, gain_one, shift_one)
    hidden_one = normed_one.astype(jnp.bfloat16)
    qkv_low = (
        jnp.dot(hidden_one, mat_qkv, preferred_element_type=jnp.float32) + bias_qkv_own
    ).astype(jnp.bfloat16)
    heads_q = qkv_low[:, :block].reshape(full_len, heads, HEAD_DIM)
    heads_k = qkv_low[:, block : 2 * block].reshape(full_len, heads, HEAD_DIM)
    heads_v = qkv_low[:, 2 * block :].reshape(full_len, heads, HEAD_DIM)
    allowed = (place_all[None, :] <= place_all[:, None]) & (seg_row[:, None] == seg_row[None, :])
    distance = (place_all[:, None] - place_all[None, :]).astype(jnp.float32)
    slopes = lax.dynamic_slice_in_dim(alibi_slopes(HEADS), own * heads, heads)
    scores = (
        jnp.einsum("qhd,khd->hqk", heads_q, heads_k, preferred_element_type=jnp.float32)
        * score_scale
        - slopes[:, None, None] * distance[None]
    )
    scores = jnp.where(allowed[None], scores, masked_score)
    row_max = jnp.max(scores, axis=-1, keepdims=True)
    exp_scores = jnp.exp(scores - row_max)
    probs_vals = exp_scores / jnp.sum(exp_scores, axis=-1, keepdims=True)
    probs_low = probs_vals.astype(jnp.bfloat16)
    attn_mix = jnp.einsum("hqk,khd->qhd", probs_low, heads_v, preferred_element_type=jnp.float32)
    attn_mix = attn_mix.reshape(full_len, block).astype(jnp.bfloat16)
    attn_part = jnp.dot(attn_mix, mat_out, preferred_element_type=jnp.float32)
    attn_out = lax.psum_scatter(
        attn_part.astype(jnp.bfloat16), "ctx", scatter_dimension=0, tiled=True
    )
    rows_loc = tokens_loc.astype(jnp.float32)
    resid_one = rows_loc + (attn_out.astype(jnp.float32) + bias_out)

    normed_two, ln_two_pull = jax.vjp(layer_norm, resid_one, gain_two, shift_two)
    hidden_two = lax.all_gather(normed_two.astype(jnp.bfloat16), "ctx", axis=0, tiled=True)
    up_pre = jnp.dot(hidden_two, mat_up, preferred_element_type=jnp.float32) + bias_up_own
    act_out, gelu_pull = jax.vjp(gelu_tanh, up_pre)
    act_low = act_out.astype(jnp.bfloat16)
    grad_act = times_trans(dy_all, mat_down)
    grad_up_low = gelu_pull(grad_act)[0].astype(jnp.bfloat16)
    grad_normed_part = times_trans(grad_up_low, mat_up).astype(jnp.bfloat16)
    grad_normed_two = lax.psum_scatter(grad_normed_part, "ctx", scatter_dimension=0, tiled=True)
    dy_loc = jnp.where(live_loc[:, None], grads_loc, jnp.zeros_like(grads_loc)).astype(jnp.float32)
    grad_bias_down = jnp.sum(dy_loc, axis=0)
    grad_bias_up = jnp.sum(grad_up_low.astype(jnp.float32), axis=0)
    grad_resid_ln, grad_gain_two, grad_shift_two = ln_two_pull(grad_normed_two.astype(jnp.float32))
    grad_resid = dy_loc + grad_resid_ln
    grad_attn_loc = grad_resid.astype(jnp.bfloat16)
    grad_bias_out = jnp.sum(grad_attn_loc.astype(jnp.float32), axis=0)
    grad_attn = lax.all_gather(grad_attn_loc, "ctx", axis=0, tiled=True)

    down_part = jnp.dot(act_low, mat_down, preferred_element_type=jnp.float32).astype(jnp.bfloat16)
    grad_attn, down_part = lax.optimization_barrier((grad_attn, down_part))
    down_out = lax.psum_scatter(down_part, "ctx", scatter_dimension=0, tiled=True)
    block_out = (resid_one + (down_out.astype(jnp.float32) + bias_down)).astype(jnp.bfloat16)[None]
    sum_up, sum_down = reduce_all(
        [
            outer_sum(hidden_two, grad_up_low)
            .astype(jnp.bfloat16)
            .reshape(parts, group, rows_in, hid),
            outer_sum(act_low, dy_all)
            .astype(jnp.bfloat16)
            .reshape(group, parts, -1, MODEL_WIDTH),
        ],
        (True, False),
        group,
        1,
    )

    grad_mixed = times_trans(grad_attn, mat_out).astype(jnp.bfloat16)
    grad_mixed = grad_mixed.reshape(full_len, heads, HEAD_DIM)
    grad_value = jnp.einsum(
        "hqk,qhd->khd", probs_low, grad_mixed, preferred_element_type=jnp.float32
    )
    grad_probs = jnp.einsum("qhd,khd->hqk", grad_mixed, heads_v, preferred_element_type=jnp.float32)
    grad_scores = probs_vals * (
        grad_probs - jnp.sum(probs_vals * grad_probs, axis=-1, keepdims=True)
    )
    grad_scores_low = grad_scores.astype(jnp.bfloat16)
    grad_query = (
        jnp.einsum("hqk,khd->qhd", grad_scores_low, heads_k, preferred_element_type=jnp.float32)
        * score_scale
    )
    grad_key = (
        jnp.einsum("hqk,qhd->khd", grad_scores_low, heads_q, preferred_element_type=jnp.float32)
        * score_scale
    )
    grad_qkv_low = jnp.concatenate(
        [part.reshape(full_len, block) for part in (grad_query, grad_key, grad_value)], axis=1
    ).astype(jnp.bfloat16)
    grad_bias_qkv = jnp.sum(grad_qkv_low.astype(jnp.float32), axis=0)
    grad_first_part = times_trans(grad_qkv_low, mat_qkv).astype(jnp.bfloat16)
    grad_normed_one = lax.psum_scatter(grad_first_part, "ctx", scatter_dimension=0, tiled=True)
    _, ln_one_pull = jax.vjp(layer_norm, rows_loc, gain_one, shift_one)
    grad_rows_ln, grad_gain_one, grad_shift_one = ln_one_pull(grad_normed_one.astype(jnp.float32))
    tokens_grad = (grad_resid + grad_rows_ln)[None]

    def own_columns(values, count):
        wide_all = jnp.zeros((count, parts, values.size // count), jnp.float32)
        return lax.dynamic_update_slice(
            wide_all, values.reshape(count, 1, -1), (0, own, 0)
        ).reshape(-1)

    grad_vec = jnp.concatenate(
        [
            grad_gain_one,
            grad_shift_one,
            own_columns(grad_bias_qkv, 3),
            grad_bias_out,
            grad_gain_two,
            grad_shift_two,
            own_columns(grad_bias_up, 1),
            grad_bias_down,
        ]
    )
    vec_pack = jnp.pad(
        grad_vec.reshape(parts, group, vec_len), ((0, 0), (0, 0), (0, 2048 - vec_len))
    ).reshape(parts, group, 16, 128)
    sum_qkv, sum_out = reduce_all(
        [
            outer_sum(hidden_one, grad_qkv_low)
            .astype(jnp.bfloat16)
            .reshape(parts, group, rows_in, wide_qkv),
            outer_sum(attn_mix, grad_attn)
            .astype(jnp.bfloat16)
            .reshape(group, 2, rows_out // 2, MODEL_WIDTH),
        ],
        (True, False),
        group,
        2,
    )
    (sum_vec,) = reduce_all([vec_pack.astype(jnp.bfloat16)], (True,), group, 3)

    ffn_cols = lax.all_to_all(sum_up, "ctx", 0, 0)
    total_up = ffn_cols.transpose(1, 0, 2).reshape(w_up.shape).astype(jnp.float32)
    total_down = sum_down.reshape(w_down.shape).astype(jnp.float32)
    total_out = sum_out.reshape(w_attn_out.shape).astype(jnp.float32)
    qkv_cols = lax.all_to_all(sum_qkv, "ctx", 0, 0)
    vec_cols = lax.all_to_all(sum_vec, "ctx", 0, 0)
    total_qkv = (
        qkv_cols.reshape(parts, rows_in, 3, block)
        .transpose(1, 2, 0, 3)
        .reshape(w_qkv.shape)
        .astype(jnp.float32)
    )
    total_vec = jnp.sum(vec_cols.astype(jnp.float32), axis=0).reshape(-1)[:vec_len]
    new_qkv, mom_qkv, sec_qkv = adamw_update(
        w_qkv, total_qkv, momentum_qkv_weight, second_qkv, 0.05, 0.1
    )
    new_out, mom_out, sec_out = adamw_update(
        w_attn_out, total_out, momentum_attn_output, second_attn_out, 0.05, 0.1
    )
    new_up, mom_up, sec_up = adamw_update(w_up, total_up, momentum_up_weight, second_up, 0.05, 0.1)
    new_down, mom_down, sec_down = adamw_update(
        w_down, total_down, momentum_down_weight, second_down, 0.05, 0.1
    )
    new_vec, mom_vec, sec_vec = adamw_update(
        vectors, total_vec, momentum_vector_rows, second_vectors, 0.6, 0.0
    )
    return (
        block_out,
        tokens_grad,
        new_qkv,
        new_out,
        new_up,
        new_down,
        new_vec,
        mom_qkv,
        mom_out,
        mom_up,
        mom_down,
        mom_vec,
        sec_qkv,
        sec_out,
        sec_up,
        sec_down,
        sec_vec,
    )


def solution(mesh):
    placed = (
        P(("fsdp", "replica"), "ctx", None),
        P(("fsdp", "replica"), "ctx", None),
        P(("fsdp", "replica"), None),
        P(("fsdp", "replica")),
        P(("ctx", "fsdp"), None),
        P(("ctx", "fsdp"), None),
        P(("ctx", "fsdp"), None),
        P(("ctx", "fsdp"), None),
        P(("ctx", "fsdp")),
        P(("ctx", "fsdp"), None),
        P(("ctx", "fsdp"), None),
        P(("ctx", "fsdp"), None),
        P(("ctx", "fsdp"), None),
        P(("ctx", "fsdp")),
        P(("ctx", "fsdp"), None),
        P(("ctx", "fsdp"), None),
        P(("ctx", "fsdp"), None),
        P(("ctx", "fsdp"), None),
        P(("ctx", "fsdp")),
    )
    return jax.shard_map(
        shards,
        mesh=mesh,
        in_specs=placed,
        out_specs=(
            P(("fsdp", "replica"), "ctx", None),
            P(("fsdp", "replica"), "ctx", None),
            P(("ctx", "fsdp"), None),
            P(("ctx", "fsdp"), None),
            P(("ctx", "fsdp"), None),
            P(("ctx", "fsdp"), None),
            P(("ctx", "fsdp")),
            P(("ctx", "fsdp"), None),
            P(("ctx", "fsdp"), None),
            P(("ctx", "fsdp"), None),
            P(("ctx", "fsdp"), None),
            P(("ctx", "fsdp")),
            P(("ctx", "fsdp"), None),
            P(("ctx", "fsdp"), None),
            P(("ctx", "fsdp"), None),
            P(("ctx", "fsdp"), None),
            P(("ctx", "fsdp")),
        ),
        check_vma=False,
    )
```
